256 devices in a mesh: slab: 64 (over y, z, core), band: 4 (over x).
Axes of the slice: x: 4, y: 4, z: 8, core: 2. Of those that a mesh axis runs over, the one named last changes fastest.
Arguments:
- wavefunctions: bfloat16 [8, 2, 256, 256, 256], P('band', None, 'slab'), may hold values from -6 to 6
- potential: float32 [256, 256, 256], P('slab', 'band'), may hold values from -0.6 to 0.6
- atom_box: int32 [3, 2048], P(None, 'slab'), may hold values from 0 to 255, as said below
- atom_count: int32 [64], P('slab'), may hold values from 8 to 32, as said below
- projectors: bfloat16 [2048, 8, 1728], P('slab'), may hold values from -0.59765625 to 0.59765625
- coupling: float32 [8, 8], replicated, may hold values from -2 to 2
Outputs:
- applied: bfloat16 [8, 2, 256, 256, 256], P('band', None, 'slab')
The draws below stay inside these ranges and needn't reach their ends.
Inputs may be any that keep to these rules, and one draw needn't show every extreme that they name: `atom_box`: atoms are laid out by owner slab, 32 slots each; row 0 of an atom's column lies among the 4 z planes of its owner slab; rows 1 and 2 are any y and x cells; boxes wrap around the periodic grid. `atom_count`: slots at and beyond the count are not live; the slabs around one defect position are full.
All inputs are finite; a program needn't handle non-finite values.
Results may differ from the reference program's by a relative error of at most 0.011.
Values may be sent and summed in bfloat16 or wider, within the bound.
No kernel may reach another device: no remote copies, remote signals or barrier semaphores. Data moves between devices by JAX's collectives and lax.ppermute only.
A program may use at most 256 MiB of HBM per device.

```python
import math
import jax
import jax.numpy as jnp
from jax import lax

NG = 256
NPROJ = 8
BOX = 12
ATOM_CAP = 32
ZS = 4
BANDS = 8
ATOMS = 2048


def draw_wavefunctions(key, part):
    key = jax.random.fold_in(key, 11)
    shape = (BANDS, 2, NG, NG, NG)
    values = jax.random.normal(key, shape, jnp.float32)
    return jnp.clip(values, -6.0, 6.0).astype(jnp.bfloat16)


def draw_atom_box(key, part):
    key = jax.random.fold_in(key, 3)
    key_plane, key_row, key_column = jax.random.split(key, 3)
    owner = jnp.arange(ATOMS, dtype=jnp.int32) // ATOM_CAP
    planes = owner * ZS + jax.random.randint(key_plane, (ATOMS,), 0, ZS, dtype=jnp.int32)
    row_start = jax.random.randint(key_row, (ATOMS,), 0, NG, dtype=jnp.int32)
    column_start = jax.random.randint(key_column, (ATOMS,), 0, NG, dtype=jnp.int32)
    return jnp.stack([planes, row_start, column_start]).astype(jnp.int32)


def draw_atom_count(key, part):
    key = jax.random.fold_in(key, 7)
    key_center, key_base = jax.random.split(key, 2)
    slab_total = ATOMS // ATOM_CAP
    center = jax.random.randint(key_center, (), 0, slab_total, dtype=jnp.int32)
    slab_ids = jnp.arange(slab_total, dtype=jnp.int32)
    distance = jnp.minimum((slab_ids - center) % slab_total, (center - slab_ids) % slab_total)
    base = jax.random.randint(key_base, (slab_total,), ATOM_CAP // 4, ATOM_CAP // 2 + 1, dtype=jnp.int32)
    return jnp.where(distance <= 1, ATOM_CAP, base).astype(jnp.int32)


def block_scale(key, shape, pieces, smallest, largest):
    def one(dim, parts):
        heights = jax.random.uniform(jax.random.fold_in(jax.random.fold_in(key, 6), dim), (parts,), jnp.float32, smallest / len(pieces), largest / len(pieces))
        return jnp.repeat(jnp.exp(heights), shape[dim] // parts).reshape((-1,) + (1,) * (len(shape) - dim - 1))

    level = one(*pieces[0])
    for cut in pieces[1:]:
        level = level * one(*cut)
    return level


def gaussian(stream_key, shape, spread, bound, cuts=(), kind=jnp.bfloat16):
    drawn = spread * jax.random.normal(stream_key, shape, jnp.float32)
    if cuts:
        drawn = drawn * block_scale(stream_key, shape, cuts, -0.22, 0.18)
    return jnp.clip(drawn, -bound, bound).astype(kind)


def setup_inputs(seed: int = 0) -> dict:
    splits = jax.random.split(jax.random.key(seed), 7)
    wavefunctions = draw_wavefunctions(jax.random.fold_in(splits[6], 71), 0)
    potential = gaussian(splits[1], (NG, NG, NG), 0.1, 0.6, ((0, 64), (1, 4)), jnp.float32)
    atom_box = draw_atom_box(jax.random.fold_in(splits[6], 71), 0)
    atom_count = draw_atom_count(jax.random.fold_in(splits[6], 71), 0)
    projectors = gaussian(splits[4], (ATOMS, NPROJ, BOX ** 3), 0.1, 0.59765625, ((0, 64),))
    coupling = gaussian(splits[5], (NPROJ, NPROJ), NPROJ ** -0.5, 2.0, (), jnp.float32)
    return {"wavefunctions": wavefunctions, "potential": potential, "atom_box": atom_box, "atom_count": atom_count, "projectors": projectors, "coupling": coupling}


def dft_table(length, sign):
    counter = jnp.arange(length, dtype=jnp.int32)
    product = counter[:, None] * counter[None, :] % length
    angle = product.astype(jnp.float32) * (2.0 * math.pi / length)
    cosine = jnp.cos(angle) / math.sqrt(length)
    sine = sign * jnp.sin(angle) / math.sqrt(length)
    return jnp.stack([jnp.stack([cosine, sine]), jnp.stack([-sine, cosine])]).astype(jnp.bfloat16)

def frequency_square(counter, length):
    signed = jnp.where(counter < length // 2, counter, counter - length)
    return (signed * signed).astype(jnp.float32)

def box_index(anchor, extent, length):
    return (anchor[:, None] + jnp.arange(extent, dtype=jnp.int32)[None, :]) % length

def reference(wavefunctions, potential, atom_box, atom_count, projectors, coupling):
    highest = lax.Precision.HIGHEST
    forward = dft_table(NG, 1.0).astype(jnp.float32)
    inverse = dft_table(NG, -1.0).astype(jnp.float32)
    counter = jnp.arange(NG, dtype=jnp.int32)
    square = frequency_square(counter, NG)
    factor = (square[:, None, None] + square[None, :, None] + square[None, None, :]) / (3.0 * (NG // 2) ** 2)
    plane_index = box_index(atom_box[0], BOX, NG)
    row_index = box_index(atom_box[1], BOX, NG)
    column_index = box_index(atom_box[2], BOX, NG)
    atom_ids = jnp.arange(ATOMS, dtype=jnp.int32)
    owner = atom_ids // ATOM_CAP
    live = (atom_ids % ATOM_CAP < atom_count[owner]).astype(jnp.float32)
    symmetric = (coupling + coupling.T) * 0.5
    weights = projectors.astype(jnp.float32)
    plane_sel = plane_index[:, :, None, None]
    row_sel = row_index[:, None, :, None]
    column_sel = column_index[:, None, None, :]

    def one_band(wave):
        field = wave.astype(jnp.float32)
        along_x = jnp.einsum('ackn,czyn->azyk', forward, field).astype(jnp.bfloat16)
        along_xy = jnp.einsum('ackn,cznx->azkx', forward, along_x.astype(jnp.float32)).astype(jnp.bfloat16)
        spectral = (jnp.einsum('ackn,cnyx->akyx', forward, along_xy.astype(jnp.float32)) * factor).astype(jnp.bfloat16)
        back_z = jnp.einsum('ackn,cnyx->akyx', inverse, spectral.astype(jnp.float32)).astype(jnp.bfloat16)
        back_zy = jnp.einsum('ackn,cznx->azkx', inverse, back_z.astype(jnp.float32)).astype(jnp.bfloat16)
        kinetic = jnp.einsum('ackn,czyn->azyk', inverse, back_zy.astype(jnp.float32))
        boxes = field[:, plane_sel, row_sel, column_sel].reshape(2, ATOMS, BOX ** 3)
        projections = jnp.einsum('apn,can->apc', weights, boxes, precision=highest)
        coefficients = live[:, None, None] * jnp.einsum('pq,aqc->apc', symmetric, projections, precision=highest)
        contrib = jnp.einsum('apn,apc->can', weights, coefficients, precision=highest)
        contrib = contrib.reshape(2, ATOMS, BOX, BOX, BOX)
        beyond = jnp.zeros((2, NG, NG, NG), jnp.float32).at[:, plane_sel, row_sel, column_sel].add(contrib)
        return (kinetic + potential[None] * field + beyond).astype(jnp.bfloat16)
    return lax.map(one_band, wavefunctions)
```

```python
import numpy as np

import jax
import jax.numpy as jnp
from jax import lax
from jax.experimental import pallas as pl
from jax.experimental.pallas import tpu as pltpu
from jax.sharding import PartitionSpec as P

BOX = 12
PAD = 16
LANES = 128
HEAP = LANES // PAD
F32 = jnp.float32
BF16 = jnp.bfloat16
HIGHEST = lax.Precision.HIGHEST
VMEM_LIMIT = 56 * 1024 * 1024
NT = (((1,), (1,)), ((), ()))
TN = (((0,), (0,)), ((), ()))


def kinetic_table(length):
    counter = np.arange(length)
    signed = np.where(counter < length // 2, counter, counter - length).astype(np.float64)
    angle = 2.0 * np.pi * ((counter[:, None] * counter[None, :]) % length) / length
    spectrum = signed**2 / (3.0 * (length // 2) ** 2)
    row = (np.cos(angle) * spectrum[None, :]).sum(1) / length
    table = row[(counter[:, None] - counter[None, :]) % length]
    high = jnp.asarray(table, F32).astype(BF16)
    low = (jnp.asarray(table, F32) - high.astype(F32)).astype(BF16)
    return high, low


def whole(space=pltpu.VMEM):
    return pl.BlockSpec(memory_space=space)


def dot(a, b, dims=None, precision=None):
    if dims is None:
        dims = (((1,), (0,)), ((), ()))
    return lax.dot_general(a, b, dims, precision=precision, preferred_element_type=F32)


def along_z_kernel(high_ref, low_ref, in_ref, out_ref, wide, result):
    length = high_ref.shape[0]
    stride = in_ref.shape[0] // length
    wide[...] = in_ref[...].astype(F32)

    def step(i, carry):
        left = wide[pl.ds(2 * i, length, stride=stride), :]
        right = wide[pl.ds(2 * i + 1, length, stride=stride), :]
        both = jnp.concatenate([left, right], axis=1).astype(BF16)
        out = dot(high_ref[...], both) + dot(low_ref[...], both)
        result[pl.ds(2 * i, length, stride=stride), :] = out[:, :LANES]
        result[pl.ds(2 * i + 1, length, stride=stride), :] = out[:, LANES:]
        return carry

    lax.fori_loop(0, stride // 2, step, 0)
    out_ref[...] = result[...].astype(BF16)


def along_z(high, low, block):
    rows = block.shape[0]
    return pl.pallas_call(
        along_z_kernel,
        out_shape=jax.ShapeDtypeStruct(block.shape, BF16),
        in_specs=[whole()] * 3,
        out_specs=whole(),
        scratch_shapes=[pltpu.VMEM((rows, LANES), F32), pltpu.VMEM((rows, LANES), F32)],
        compiler_params=pltpu.CompilerParams(vmem_limit_bytes=VMEM_LIMIT),
        cost_estimate=pl.CostEstimate(
            flops=4 * 256 * rows * LANES, bytes_accessed=4 * rows * LANES, transcendentals=0
        ),
        name="along_z",
    )(high, low, block)


def select_matrix(xt_ref, group, length):
    column = lax.broadcasted_iota(jnp.int32, (length, LANES), 0)
    return jnp.where(column == xt_ref[pl.ds(group, 1), :], 1.0, 0.0).astype(BF16)


def heap_matrix():
    lane = lax.broadcasted_iota(jnp.int32, (HEAP, LANES), 1)
    atom = lax.broadcasted_iota(jnp.int32, (HEAP, LANES), 0)
    return jnp.where(lane // PAD == atom, 1.0, 0.0).astype(F32)


def project_kernel(y_ref, xt_ref, wave_ref, weight_ref, out_ref, field, sums):
    reach, heaps, nproj = weight_ref.shape[1], weight_ref.shape[0], weight_ref.shape[2]
    planes, length = wave_ref.shape[0], wave_ref.shape[1]
    rows = weight_ref.shape[3]
    parts = planes * PAD // rows
    for i in range(planes):
        for half in range(2):
            part = wave_ref[i, :, half * LANES : (half + 1) * LANES].astype(F32)
            field[i, half, 0:length, :] = part
            field[i, half, length : length + PAD, :] = part[0:PAD]
    lane = lax.broadcasted_iota(jnp.int32, (planes * PAD, LANES), 1)

    def step(index, carry):
        reach_index = index // heaps
        heap = index % heaps
        select = select_matrix(xt_ref, index, length)
        taken = jnp.zeros((planes * PAD, LANES), F32)
        for a in range(HEAP):
            y0 = y_ref[index * HEAP + a]
            left = field[:, 0, pl.ds(y0, PAD), :].reshape(planes * PAD, LANES)
            right = field[:, 1, pl.ds(y0, PAD), :].reshape(planes * PAD, LANES)
            window = jnp.concatenate([left, right], axis=1).astype(BF16)
            taken = jnp.where(lane // PAD == a, dot(window, select), taken)
        lines = []
        for p in range(nproj):
            weight = weight_ref[heap, reach_index, p].astype(F32)
            for part in range(parts):
                product = weight * taken[part * rows : (part + 1) * rows]
                lines.append(jnp.sum(product, axis=0, keepdims=True))
        sums[pl.ds(pl.multiple_of(index * nproj * parts, 8), nproj * parts), :] = jnp.concatenate(lines, axis=0)
        return carry

    lax.fori_loop(0, reach * heaps, step, 0)
    per_reach = heaps * nproj * parts
    for d in range(reach):
        out_ref[d] = dot(
            heap_matrix(), sums[d * per_reach : (d + 1) * per_reach, :], NT, HIGHEST
        )


def project(y0, xt, wave, weights):
    heaps, reach, nproj, rows, _ = weights.shape
    planes, length, _ = wave.shape
    parts = planes * PAD // rows
    return pl.pallas_call(
        project_kernel,
        out_shape=jax.ShapeDtypeStruct((reach, HEAP, heaps * nproj * parts), F32),
        in_specs=[whole(pltpu.SMEM), whole(), whole(), whole()],
        out_specs=whole(),
        scratch_shapes=[
            pltpu.VMEM((planes, 2, length + PAD, LANES), F32),
            pltpu.VMEM((reach * heaps * nproj * parts, LANES), F32),
        ],
        compiler_params=pltpu.CompilerParams(vmem_limit_bytes=VMEM_LIMIT),
        cost_estimate=pl.CostEstimate(
            flops=10_000_000_000, bytes_accessed=5_000_000, transcendentals=0
        ),
        name="project",
    )(y0, xt, wave, weights)


def local_kernel(
    y_ref, xt_ref, full_ref, live_ref, mix_ref, high_ref, low_ref, potential_ref,
    wave_ref, weight_ref, out_ref, total, spread,
):
    heaps, reach, nproj, rows, _ = weight_ref.shape
    planes, length = wave_ref.shape[0], wave_ref.shape[1]
    slab_planes = potential_ref.shape[0]
    parts = planes // slab_planes
    per_reach = heaps * nproj * parts

    def fill(i, carry):
        wave = wave_ref[i]
        value = dot(wave, high_ref[...]) + dot(wave, low_ref[...])
        value += dot(high_ref[...], wave) + dot(low_ref[...], wave)
        value += potential_ref[lax.rem(i, slab_planes)].astype(F32) * wave.astype(F32)
        for half in range(2):
            total[i, half, 0:length, :] = value[:, half * LANES : (half + 1) * LANES]
            total[i, half, length : length + PAD, :] = jnp.zeros((PAD, LANES), F32)
        return carry

    lax.fori_loop(0, planes, fill, 0)
    for d in range(reach):
        coefficients = dot(full_ref[d] * live_ref[d], mix_ref[...], None, HIGHEST)
        spread[d * per_reach : (d + 1) * per_reach, :] = dot(
            coefficients, heap_matrix(), TN, HIGHEST
        )
    lane = lax.broadcasted_iota(jnp.int32, (planes * PAD, LANES), 1)

    def step(index, carry):
        reach_index = index // heaps
        heap = index % heaps
        select = select_matrix(xt_ref, index, length)
        lines = spread[pl.ds(pl.multiple_of(index * nproj * parts, 8), nproj * parts), :]
        blocks = [jnp.zeros((rows, LANES), F32) for _ in range(parts)]
        for p in range(nproj):
            weight = weight_ref[heap, reach_index, p].astype(F32)
            for part in range(parts):
                at = p * parts + part
                blocks[part] = blocks[part] + weight * lines[at : at + 1, :]
        blocks = jnp.concatenate(blocks, axis=0)
        for a in range(HEAP):
            y0 = y_ref[index * HEAP + a]
            one = jnp.where(lane // PAD == a, blocks, 0.0).astype(BF16)
            placed = dot(one, select, NT)
            for half in range(2):
                part = placed[:, half * LANES : (half + 1) * LANES]
                total[:, half, pl.ds(y0, PAD), :] += part.reshape(planes, PAD, LANES)
        return carry

    lax.fori_loop(0, reach * heaps, step, 0)

    def finish(i, carry):
        for half in range(2):
            at = slice(half * LANES, (half + 1) * LANES)
            out_ref[i, 0:PAD, at] = total[i, half, 0:PAD, :] + total[i, half, length : length + PAD, :]
            out_ref[i, PAD:length, at] = total[i, half, PAD:length, :]
        return carry

    lax.fori_loop(0, planes, finish, 0)


def local_part(y0, xt, full, live, mix, high, low, potential, wave, weights):
    heaps, reach, nproj, rows, _ = weights.shape
    planes, length, _ = wave.shape
    parts = planes * PAD // rows
    return pl.pallas_call(
        local_kernel,
        out_shape=jax.ShapeDtypeStruct(wave.shape, F32),
        in_specs=[whole(pltpu.SMEM)] + [whole()] * 9,
        out_specs=whole(),
        scratch_shapes=[
            pltpu.VMEM((planes, 2, length + PAD, LANES), F32),
            pltpu.VMEM((reach * heaps * nproj * parts, LANES), F32),
        ],
        compiler_params=pltpu.CompilerParams(vmem_limit_bytes=VMEM_LIMIT),
        cost_estimate=pl.CostEstimate(
            flops=10_000_000_000, bytes_accessed=10_000_000, transcendentals=0
        ),
        name="local",
    )(y0, xt, full, live, mix, high, low, potential, wave, weights)


def join_kernel(local_ref, arrived_ref, out_ref):
    bands, rows, columns = arrived_ref.shape[0], arrived_ref.shape[1], arrived_ref.shape[2]
    slab_planes, comps = arrived_ref.shape[3], arrived_ref.shape[4]
    for b in range(bands):
        for c in range(comps):
            for z in range(slab_planes):
                plane = (b * comps + c) * slab_planes + z
                for r in range(rows):
                    for h in range(columns):
                        at = (plane, slice(r * 16, (r + 1) * 16), slice(h * LANES, (h + 1) * LANES))
                        value = local_ref[at] + arrived_ref[b, r, h, z, c].astype(F32)
                        out_ref[at] = value.astype(BF16)


def join(local, arrived):
    bands, row_blocks, halves, slab_planes, comps = arrived.shape[:5]
    planes, length, _ = local.shape
    count = 8
    step_rows = row_blocks // count
    return pl.pallas_call(
        join_kernel,
        out_shape=jax.ShapeDtypeStruct(local.shape, BF16),
        grid=(count,),
        in_specs=[
            pl.BlockSpec((planes, length // count, length), lambda i: (0, i, 0)),
            pl.BlockSpec(
                (bands, step_rows, halves, slab_planes, comps, 16, LANES),
                lambda i: (0, i, 0, 0, 0, 0, 0),
            ),
        ],
        out_specs=pl.BlockSpec((planes, length // count, length), lambda i: (0, i, 0)),
        compiler_params=pltpu.CompilerParams(vmem_limit_bytes=VMEM_LIMIT),
        cost_estimate=pl.CostEstimate(
            flops=2 * local.size, bytes_accessed=8 * local.size, transcendentals=0
        ),
        name="join",
    )(local, arrived)


def ahead(block, distance):
    size = lax.axis_size("slab")
    return lax.ppermute(block, "slab", [(i, (i + distance) % size) for i in range(size)])


def framed_weights(projectors, atom_box, slab_anchor, slab_planes):
    nproj = projectors.shape[1]
    mine = lax.axis_index("band") * HEAP
    share = lax.dynamic_slice_in_dim(projectors, mine, HEAP, 0)
    share = share.reshape(HEAP, nproj, BOX, BOX, BOX).transpose(1, 2, 3, 0, 4)
    share = jnp.pad(share, ((0, 0), (0, 0), (0, PAD - BOX), (0, 0), (0, PAD - BOX)))
    share = share.reshape(nproj, BOX, PAD, LANES)
    offset = lax.dynamic_slice_in_dim(atom_box[0], mine, HEAP, 0) - slab_anchor
    offset = jnp.repeat(offset, PAD)
    frames = BOX + slab_planes
    framed = jnp.zeros((nproj, frames, PAD, LANES), projectors.dtype)
    for o in range(slab_planes):
        moved = jnp.pad(share, ((0, 0), (o, slab_planes - o), (0, 0), (0, 0)))
        framed = jnp.where(offset == o, moved, framed)
    reach = frames // slab_planes
    framed = framed.reshape(nproj, reach, slab_planes * PAD, LANES)
    return framed.transpose(1, 0, 2, 3)


def shards(wavefunctions, potential, atom_box, atom_count, projectors, coupling):
    bands, comps, slab_planes, length, _ = wavefunctions.shape
    parts = bands * comps
    planes = parts * slab_planes
    slabs = lax.axis_size("slab")
    slots, nproj, _ = projectors.shape
    heaps = slots // HEAP
    reach = (BOX + slab_planes) // slab_planes
    high, low = kinetic_table(length)
    slab_anchor = lax.axis_index("slab") * slab_planes

    row_blocks, halves = length // 16, length // LANES
    send = wavefunctions.reshape(bands, comps, slab_planes, row_blocks, 16, halves, LANES)
    send = send.transpose(0, 3, 5, 2, 1, 4, 6).reshape(slabs, slab_planes * comps, 16, LANES)
    columns = lax.all_to_all(send, "slab", split_axis=0, concat_axis=0, tiled=True)

    framed = framed_weights(projectors, atom_box, slab_anchor, slab_planes)
    weights = jnp.stack([framed[0]] + [ahead(framed[d], d) for d in range(1, reach)])
    weights = lax.all_gather(weights, "band", axis=0)
    facts = jnp.concatenate([atom_box[1], atom_box[2], atom_count, jnp.zeros((LANES - 2 * slots - 1,), jnp.int32)])
    facts = jnp.stack([facts] + [ahead(facts, d) for d in range(1, reach)])
    y0 = facts[:, :slots].reshape(-1)
    x0 = facts[:, slots : 2 * slots]
    count = facts[:, 2 * slots]
    k = jnp.arange(PAD, dtype=jnp.int32)
    xt = jnp.where(k < BOX, (x0[:, :, None] + k) % length, -1).reshape(reach * heaps, LANES)

    wave = wavefunctions.reshape(planes, length, length)
    partial = project(y0, xt, wave, weights)
    full = partial
    for o in range(1, reach):
        up = ahead(partial[o:], -o)
        down = ahead(partial[: reach - o], o)
        full = full + jnp.pad(up, ((0, o), (0, 0), (0, 0)))
        full = full + jnp.pad(down, ((o, 0), (0, 0), (0, 0)))

    slot = jnp.arange(heaps)[None, :] * HEAP + jnp.arange(HEAP)[:, None]
    live = (slot[None] < count[:, None, None]).astype(F32)
    live = jnp.repeat(live, nproj * parts, axis=2)
    symmetric = (coupling + coupling.T) * 0.5
    mix = jnp.einsum(
        "gh,pq,bc->gqbhpc", jnp.eye(heaps, dtype=F32), symmetric, jnp.eye(parts, dtype=F32),
        precision=HIGHEST,
    ).reshape(heaps * nproj * parts, heaps * nproj * parts)
    potential_full = lax.all_gather(potential.astype(BF16), "band", axis=1, tiled=True)
    local = local_part(y0, xt, full, live, mix, high, low, potential_full, wave, weights)

    columns = along_z(high, low, columns.reshape(-1, LANES))
    columns = columns.reshape(slabs, slab_planes * comps, 16, LANES)
    back = lax.all_to_all(columns, "slab", split_axis=0, concat_axis=0, tiled=True)
    back = back.reshape(bands, row_blocks, halves, slab_planes, comps, 16, LANES)
    return join(local, back).reshape(wavefunctions.shape)


def solution(mesh):
    placed = (
        P("band", None, "slab", None, None),
        P("slab", "band", None),
        P(None, "slab"),
        P("slab"),
        P("slab", None, None),
        P(),
    )
    return jax.shard_map(
        shards,
        mesh=mesh,
        in_specs=placed,
        out_specs=P("band", None, "slab", None, None),
        check_vma=False,
    )
```

```python
import functools

import numpy as np

import jax
import jax.numpy as jnp
from jax import lax
from jax.experimental import pallas as pl
from jax.experimental.pallas import tpu as pltpu
from jax.sharding import PartitionSpec as P

NG = 256
BOX = 12
SLAB_PLANES = 4
PAD = 16
LANES = 128
HEAP = LANES // PAD
F32 = jnp.float32
BF16 = jnp.bfloat16
HIGHEST = lax.Precision.HIGHEST
VMEM_LIMIT = 28 * 1024 * 1024
NT = (((1,), (1,)), ((), ()))
TN = (((0,), (0,)), ((), ()))


def kinetic_table(length):
    counter = np.arange(length)
    signed = np.where(counter < length // 2, counter, counter - length).astype(np.float64)
    angle = 2.0 * np.pi * ((counter[:, None] * counter[None, :]) % length) / length
    spectrum = signed**2 / (3.0 * (length // 2) ** 2)
    row = (np.cos(angle) * spectrum[None, :]).sum(1) / length
    table = row[(counter[:, None] - counter[None, :]) % length]
    high = jnp.asarray(table, F32).astype(BF16)
    low = (jnp.asarray(table, F32) - high.astype(F32)).astype(BF16)
    return high, low


def whole(space=pltpu.VMEM):
    return pl.BlockSpec(memory_space=space)


def dot(a, b, dims=None, precision=None):
    if dims is None:
        dims = (((1,), (0,)), ((), ()))
    return lax.dot_general(a, b, dims, precision=precision, preferred_element_type=F32)


def along_z_kernel(high_ref, low_ref, in_ref, *refs):
    out_ref, here, wide, result, there, in_sem, out_sem = refs[-7:]
    length = high_ref.shape[0]
    comps = here.shape[0]
    loads, stores = [], []
    for c in range(comps):
        loads.append(pltpu.make_async_copy(in_ref.at[:, c], here.at[c], in_sem.at[c]))
        stores.append(pltpu.make_async_copy(there.at[c], out_ref.at[:, c], out_sem.at[c]))
        loads[c].start()
    for c in range(comps):
        loads[c].wait()
        wide[c] = here[c].astype(F32).reshape(length * 16, LANES)
        for i in range(8):
            left = wide[c, pl.ds(2 * i, length, stride=16), :]
            right = wide[c, pl.ds(2 * i + 1, length, stride=16), :]
            both = jnp.concatenate([left, right], axis=1).astype(BF16)
            out = dot(high_ref[...], both) + dot(low_ref[...], both)
            result[c, pl.ds(2 * i, length, stride=16), :] = out[:, :LANES]
            result[c, pl.ds(2 * i + 1, length, stride=16), :] = out[:, LANES:]
        there[c] = result[c].reshape(length, 16, LANES).astype(BF16)
        stores[c].start()
    for c in range(comps):
        stores[c].wait()


def along_z(high, low, block, after):
    length, comps = block.shape[:2]
    return pl.pallas_call(
        along_z_kernel,
        out_shape=jax.ShapeDtypeStruct(block.shape, BF16),
        in_specs=[whole()] * 2 + [whole(pltpu.HBM)] + [whole(pl.ANY)] * len(after),
        out_specs=whole(pltpu.HBM),
        scratch_shapes=[
            pltpu.VMEM((comps, length, 16, LANES), BF16),
            pltpu.VMEM((comps, length * 16, LANES), F32),
            pltpu.VMEM((comps, length * 16, LANES), F32),
            pltpu.VMEM((comps, length, 16, LANES), BF16),
            pltpu.SemaphoreType.DMA((comps,)),
            pltpu.SemaphoreType.DMA((comps,)),
        ],
        compiler_params=pltpu.CompilerParams(vmem_limit_bytes=VMEM_LIMIT),
        cost_estimate=pl.CostEstimate(
            flops=4 * length * block.size, bytes_accessed=4 * block.size, transcendentals=0
        ),
        name="along_z",
    )(high, low, block, *after)


def select_matrix(facts, length):
    column = lax.broadcasted_iota(jnp.int32, (length, LANES), 0).astype(F32)
    return jnp.where(column == facts[0:1], 1.0, 0.0).astype(BF16)


def heap_matrix():
    lane = lax.broadcasted_iota(jnp.int32, (HEAP, LANES), 1)
    atom = lax.broadcasted_iota(jnp.int32, (HEAP, LANES), 0)
    return jnp.where(lane // PAD == atom, 1.0, 0.0).astype(F32)


def project_kernel(y_ref, wave_ref, cargo_ref, out_ref, field, sums, *, heaps, reach, nproj):
    planes, length = wave_ref.shape[0], wave_ref.shape[1]
    rows = SLAB_PLANES * PAD
    parts = planes // SLAB_PLANES
    stretch = nproj * rows + PAD
    for i in range(planes):
        for half in range(2):
            part = wave_ref[i, :, half * LANES : (half + 1) * LANES].astype(F32)
            field[i, half, 0:length, :] = part
            field[i, half, length : length + PAD, :] = part[0:PAD]
    lane = lax.broadcasted_iota(jnp.int32, (planes * PAD, LANES), 1)

    def step(index, carry):
        base = (index // heaps) * stretch
        heap = index % heaps
        at = pl.multiple_of(base + nproj * rows, 16)
        facts = cargo_ref[heap, pl.ds(at, PAD), :].astype(F32)
        select = select_matrix(facts, length)
        taken = jnp.zeros((planes * PAD, LANES), F32)
        for a in range(HEAP):
            y0 = y_ref[index * HEAP + a]
            left = field[:, 0, pl.ds(y0, PAD), :].reshape(planes * PAD, LANES)
            right = field[:, 1, pl.ds(y0, PAD), :].reshape(planes * PAD, LANES)
            window = jnp.concatenate([left, right], axis=1).astype(BF16)
            taken = jnp.where(lane // PAD == a, dot(window, select), taken)
        lines = []
        for p in range(nproj):
            at = pl.multiple_of(base + p * rows, 16)
            weight = cargo_ref[heap, pl.ds(at, rows), :].astype(F32)
            for part in range(parts):
                product = weight * taken[part * rows : (part + 1) * rows]
                lines.append(jnp.sum(product, axis=0, keepdims=True))
        at = pl.multiple_of(index * nproj * parts, 8)
        sums[pl.ds(at, nproj * parts), :] = jnp.concatenate(lines, axis=0)
        return carry

    lax.fori_loop(0, reach * heaps, step, 0)
    per_reach = heaps * nproj * parts
    for d in range(reach):
        out_ref[d] = dot(
            heap_matrix(), sums[d * per_reach : (d + 1) * per_reach, :], NT, HIGHEST
        )


def project(y0, wave, cargo, reach, nproj):
    heaps = cargo.shape[0]
    planes, length, _ = wave.shape
    parts = planes // SLAB_PLANES
    return pl.pallas_call(
        functools.partial(project_kernel, heaps=heaps, reach=reach, nproj=nproj),
        out_shape=jax.ShapeDtypeStruct((reach, HEAP, heaps * nproj * parts), F32),
        in_specs=[whole(pltpu.SMEM), whole(), whole()],
        out_specs=whole(),
        scratch_shapes=[
            pltpu.VMEM((planes, 2, length + PAD, LANES), F32),
            pltpu.VMEM((reach * heaps * nproj * parts, LANES), F32),
        ],
        compiler_params=pltpu.CompilerParams(vmem_limit_bytes=VMEM_LIMIT),
        cost_estimate=pl.CostEstimate(
            flops=10_000_000_000, bytes_accessed=5_000_000, transcendentals=0
        ),
        name="project",
    )(y0, wave, cargo)


def local_kernel(
    y_ref, partial_ref, mix_ref, high_ref, low_ref, wave_ref, cargo_ref, after_ref, *refs, reach, nproj
):
    out_ref, total, spread, well = refs[-4:]
    ups, downs = refs[0 : reach - 1], refs[reach - 1 : 2 * (reach - 1)]
    heaps = cargo_ref.shape[0]
    planes, length = wave_ref.shape[0], wave_ref.shape[1]
    rows = SLAB_PLANES * PAD
    parts = planes // SLAB_PLANES
    stretch = nproj * rows + PAD
    per_reach = heaps * nproj * parts
    share = length // heaps

    for r in range(heaps):
        place = lax.rem(y_ref[reach * heaps * HEAP] + r, heaps) * share
        for half in range(2):
            for z in range(SLAB_PLANES):
                at = reach * stretch + (half * SLAB_PLANES + z) * share
                well[half, z, pl.ds(pl.multiple_of(place, 16), share), :] = cargo_ref[r, at : at + share, :].astype(F32)

    def fill(i, carry):
        wave = wave_ref[i]
        value = dot(wave, high_ref[...]) + dot(wave, low_ref[...])
        value += dot(high_ref[...], wave) + dot(low_ref[...], wave)
        wide = wave.astype(F32)
        for half in range(2):
            at = slice(half * LANES, (half + 1) * LANES)
            potential = well[half, lax.rem(i, SLAB_PLANES)]
            total[i, half, 0:length, :] = value[:, at] + potential * wide[:, at]
            total[i, half, length : length + PAD, :] = jnp.zeros((PAD, LANES), F32)
        return carry

    lax.fori_loop(0, planes, fill, 0)
    for d in range(reach):
        full = partial_ref[d]
        for o in range(1, reach):
            if d + o < reach:
                full = full + ups[o - 1][d]
            if d >= o:
                full = full + downs[o - 1][d - o]
        coefficients = dot(full, mix_ref[...], None, HIGHEST)
        spread[d * per_reach : (d + 1) * per_reach, :] = dot(
            coefficients, heap_matrix(), TN, HIGHEST
        )
    lane = lax.broadcasted_iota(jnp.int32, (planes * PAD, LANES), 1)

    def step(index, carry):
        base = (index // heaps) * stretch
        heap = index % heaps
        at = pl.multiple_of(base + nproj * rows, 16)
        facts = cargo_ref[heap, pl.ds(at, PAD), :].astype(F32)
        select = select_matrix(facts, length)
        at = pl.multiple_of(index * nproj * parts, 8)
        lines = spread[pl.ds(at, nproj * parts), :] * facts[2:3]
        blocks = [jnp.zeros((rows, LANES), F32) for _ in range(parts)]
        for p in range(nproj):
            at = pl.multiple_of(base + p * rows, 16)
            weight = cargo_ref[heap, pl.ds(at, rows), :].astype(F32)
            for part in range(parts):
                at = p * parts + part
                blocks[part] = blocks[part] + weight * lines[at : at + 1, :]
        blocks = jnp.concatenate(blocks, axis=0)
        for a in range(HEAP):
            y0 = y_ref[index * HEAP + a]
            one = jnp.where(lane // PAD == a, blocks, 0.0).astype(BF16)
            placed = dot(one, select, NT)
            for half in range(2):
                part = placed[:, half * LANES : (half + 1) * LANES]
                total[:, half, pl.ds(y0, PAD), :] += part.reshape(planes, PAD, LANES)
        return carry

    lax.fori_loop(0, reach * heaps, step, 0)

    def finish(i, carry):
        for half in range(2):
            at = slice(half * LANES, (half + 1) * LANES)
            out_ref[i, 0:PAD, at] = total[i, half, 0:PAD, :] + total[i, half, length : length + PAD, :]
            out_ref[i, PAD:length, at] = total[i, half, PAD:length, :]
        return carry

    lax.fori_loop(0, planes, finish, 0)


def local_part(y0, partial, mix, high, low, wave, cargo, after, ups, downs, nproj):
    heaps = cargo.shape[0]
    planes, length, _ = wave.shape
    parts = planes // SLAB_PLANES
    reach = partial.shape[0]
    return pl.pallas_call(
        functools.partial(local_kernel, reach=reach, nproj=nproj),
        out_shape=jax.ShapeDtypeStruct(wave.shape, F32),
        in_specs=[whole(pltpu.SMEM)] + [whole()] * 6 + [whole(pl.ANY)] + [whole()] * (2 * reach - 2),
        out_specs=whole(),
        scratch_shapes=[
            pltpu.VMEM((planes, 2, length + PAD, LANES), F32),
            pltpu.VMEM((reach * heaps * nproj * parts, LANES), F32),
            pltpu.VMEM((2, SLAB_PLANES, length, LANES), F32),
        ],
        compiler_params=pltpu.CompilerParams(vmem_limit_bytes=VMEM_LIMIT),
        cost_estimate=pl.CostEstimate(
            flops=10_000_000_000, bytes_accessed=10_000_000, transcendentals=0
        ),
        name="local",
    )(y0, partial, mix, high, low, wave, cargo, after, *ups, *downs)


def pack_kernel(in_ref, after_ref, out_ref):
    bands, rows, columns, slab_planes, comps = out_ref.shape[:5]
    for b in range(bands):
        for c in range(comps):
            for z in range(slab_planes):
                plane = (b * comps + c) * slab_planes + z
                for r in range(rows):
                    for h in range(columns):
                        at = (plane, slice(r * 16, (r + 1) * 16), slice(h * LANES, (h + 1) * LANES))
                        out_ref[b, r, h, z, c] = in_ref[at]


def pack(wave, bands, after):
    planes, length, _ = wave.shape
    comps = planes // SLAB_PLANES // bands
    count = 4
    row_blocks, halves = length // 16, length // LANES
    shape = (bands, row_blocks, halves, SLAB_PLANES, comps, 16, LANES)
    return pl.pallas_call(
        pack_kernel,
        out_shape=jax.ShapeDtypeStruct(shape, BF16),
        grid=(count,),
        in_specs=[
            pl.BlockSpec((planes, length // count, length), lambda i: (0, i, 0)),
            whole(pl.ANY),
        ],
        out_specs=pl.BlockSpec(
            (bands, row_blocks // count) + shape[2:], lambda i: (0, i, 0, 0, 0, 0, 0)
        ),
        compiler_params=pltpu.CompilerParams(vmem_limit_bytes=VMEM_LIMIT),
        cost_estimate=pl.CostEstimate(flops=0, bytes_accessed=4 * wave.size, transcendentals=0),
        name="pack",
    )(wave, after)


def frame_kernel(where_ref, box_ref, count_ref, share_ref, out_ref, dense):
    heap = share_ref.shape[0]
    nproj, cells = share_ref.shape[1], BOX * BOX
    band, anchor = where_ref[0], where_ref[1] * SLAB_PLANES
    line = lax.broadcasted_iota(jnp.int32, (cells, LANES), 0)
    lane = lax.broadcasted_iota(jnp.int32, (cells, LANES), 1)
    pick = jnp.where(line % BOX == lane % PAD, 1.0, 0.0).astype(BF16)
    row = lax.broadcasted_iota(jnp.int32, (PAD, cells), 0)
    cell = lax.broadcasted_iota(jnp.int32, (PAD, cells), 1)
    on_row = cell // BOX == row
    lane = lax.broadcasted_iota(jnp.int32, (nproj * PAD, LANES), 1)

    def one_atom(a, carry):
        values = share_ref[a].astype(F32)
        for i in range(BOX):
            part = values[:, i * cells : (i + 1) * cells]
            part = jnp.where(on_row[None], part[:, None, :], 0.0)
            part = part.reshape(nproj * PAD, cells).astype(BF16)
            dense[i] = jnp.where(lane // PAD == a, dot(part, pick), dense[i])
        return carry

    dense[...] = jnp.zeros_like(dense)
    lax.fori_loop(0, heap, one_atom, 0)

    lane = lax.broadcasted_iota(jnp.int32, (1, LANES), 1)
    offset = jnp.zeros((1, LANES), jnp.int32)
    row0 = jnp.zeros((1, LANES), jnp.int32)
    column0 = jnp.zeros((1, LANES), jnp.int32)
    live = jnp.zeros((1, LANES), F32)
    for a in range(heap):
        slot = band * heap + a
        mine = lane // PAD == a
        offset = jnp.where(mine, box_ref[0, slot] - anchor, offset)
        row0 = jnp.where(mine, box_ref[1, slot], row0)
        column0 = jnp.where(mine, box_ref[2, slot], column0)
        live = jnp.where(mine, jnp.where(slot < count_ref[0], 1.0, 0.0), live)
    k = lane % PAD
    target = jnp.where(k < BOX, (column0 + k) % NG, -1)
    facts = jnp.concatenate(
        [target.astype(F32), row0.astype(F32), live, jnp.zeros((PAD - 3, LANES), F32)], axis=0
    ).astype(BF16)

    rows = SLAB_PLANES * PAD
    for f in range(BOX + SLAB_PLANES):
        d, z = f // SLAB_PLANES, f % SLAB_PLANES
        framed = jnp.zeros((nproj * PAD, LANES), F32)
        for o in range(SLAB_PLANES):
            if 0 <= f - o < BOX:
                framed = jnp.where(offset == o, dense[f - o], framed)
        framed = framed.astype(BF16)
        for p in range(nproj):
            out_ref[d, p * rows + z * PAD : p * rows + (z + 1) * PAD, :] = framed[p * PAD : (p + 1) * PAD]
    for d in range(out_ref.shape[0]):
        out_ref[d, nproj * rows : nproj * rows + PAD, :] = facts


def frame(projectors, atom_box, atom_count):
    _, nproj, cells = projectors.shape
    reach = (BOX + SLAB_PLANES) // SLAB_PLANES
    where = jnp.stack([lax.axis_index("band"), lax.axis_index("slab")]).astype(jnp.int32)
    shape = (reach, nproj * SLAB_PLANES * PAD + PAD, LANES)
    return pl.pallas_call(
        frame_kernel,
        out_shape=jax.ShapeDtypeStruct(shape, BF16),
        grid_spec=pltpu.PrefetchScalarGridSpec(
            num_scalar_prefetch=3,
            grid=(1,),
            in_specs=[pl.BlockSpec((HEAP, nproj, cells), lambda i, where, box, count: (where[0], 0, 0))],
            out_specs=pl.BlockSpec(shape, lambda i, where, box, count: (0, 0, 0)),
            scratch_shapes=[pltpu.VMEM((BOX, nproj * PAD, LANES), F32)],
        ),
        compiler_params=pltpu.CompilerParams(vmem_limit_bytes=VMEM_LIMIT),
        cost_estimate=pl.CostEstimate(
            flops=1_000_000_000, bytes_accessed=1_000_000, transcendentals=0
        ),
        name="frame",
    )(where, atom_box, atom_count, projectors)


def join_kernel(local_ref, arrived_ref, out_ref, here, there, in_sem, out_sem):
    bands, rows, columns, slab_planes, comps = arrived_ref.shape[:5]
    count = in_sem.shape[0]
    step = rows // count
    loads, stores = [], []
    for i in range(count):
        at = slice(i * step, (i + 1) * step)
        lines = slice(i * step * 16, (i + 1) * step * 16)
        loads.append(pltpu.make_async_copy(arrived_ref.at[:, at], here.at[:, at], in_sem.at[i]))
        stores.append(pltpu.make_async_copy(there.at[:, lines], out_ref.at[:, lines], out_sem.at[i]))
        loads[i].start()
    for i in range(count):
        loads[i].wait()
        for r in range(i * step, (i + 1) * step):
            for b in range(bands):
                for c in range(comps):
                    for z in range(slab_planes):
                        plane = (b * comps + c) * slab_planes + z
                        for h in range(columns):
                            at = (plane, slice(r * 16, (r + 1) * 16), slice(h * LANES, (h + 1) * LANES))
                            there[at] = (local_ref[at] + here[b, r, h, z, c].astype(F32)).astype(BF16)
        stores[i].start()
    for i in range(count):
        stores[i].wait()


def join(local, arrived):
    count = 8
    return pl.pallas_call(
        join_kernel,
        out_shape=jax.ShapeDtypeStruct(local.shape, BF16),
        in_specs=[whole(), whole(pltpu.HBM)],
        out_specs=whole(pltpu.HBM),
        scratch_shapes=[
            pltpu.VMEM(arrived.shape, BF16),
            pltpu.VMEM(local.shape, BF16),
            pltpu.SemaphoreType.DMA((count,)),
            pltpu.SemaphoreType.DMA((count,)),
        ],
        compiler_params=pltpu.CompilerParams(vmem_limit_bytes=VMEM_LIMIT),
        cost_estimate=pl.CostEstimate(
            flops=2 * local.size, bytes_accessed=8 * local.size, transcendentals=0
        ),
        name="join",
    )(local, arrived)


def ahead(block, distance, axis="slab"):
    size = lax.axis_size(axis)
    return lax.ppermute(block, axis, [(i, (i + distance) % size) for i in range(size)])


def shards(wavefunctions, potential, atom_box, atom_count, projectors, coupling):
    bands, comps, slab_planes, length, _ = wavefunctions.shape
    parts = bands * comps
    planes = parts * slab_planes
    slabs = lax.axis_size("slab")
    heaps = lax.axis_size("band")
    nproj = projectors.shape[1]
    high, low = kinetic_table(length)
    wave = wavefunctions.reshape(planes, length, length)

    framed = frame(projectors, atom_box, atom_count)
    reach = framed.shape[0]
    arrived = [framed[0]] + [ahead(framed[d], d) for d in range(1, reach)]

    send = pack(wave, bands, arrived[1]).reshape(slabs, slab_planes * comps, 16, LANES)
    columns = lax.all_to_all(send, "slab", split_axis=0, concat_axis=0, tiled=True)

    well = potential.astype(BF16).reshape(slab_planes, length // heaps, 2, LANES)
    well = well.transpose(2, 0, 1, 3).reshape(-1, LANES)
    cargo = jnp.concatenate(arrived + [well], axis=0)
    cargo = jnp.stack([cargo] + [ahead(cargo, -r, "band") for r in range(1, heaps)])
    stretch = framed.shape[1]
    tops = jnp.stack([cargo[:, d * stretch + stretch - PAD + 1, ::PAD] for d in range(reach)])
    y0 = jnp.concatenate([tops.astype(jnp.int32).reshape(-1), lax.axis_index("band").astype(jnp.int32)[None]])

    partial = project(y0, wave, cargo, reach, nproj)
    ups = [ahead(partial[o:], -o) for o in range(1, reach)]
    downs = [ahead(partial[: reach - o], o) for o in range(1, reach)]

    symmetric = (coupling + coupling.T) * 0.5
    mix = jnp.einsum(
        "gh,pq,bc->gqbhpc", jnp.eye(heaps, dtype=F32), symmetric, jnp.eye(parts, dtype=F32),
        precision=HIGHEST,
    ).reshape(heaps * nproj * parts, heaps * nproj * parts)

    columns = along_z(high, low, columns.reshape(length, comps, 16, LANES), ups + downs)
    local = local_part(y0, partial, mix, high, low, wave, cargo, columns, ups, downs, nproj)
    columns = columns.reshape(slabs, slab_planes * comps, 16, LANES)
    back = lax.all_to_all(columns, "slab", split_axis=0, concat_axis=0, tiled=True)
    back = back.reshape(bands, length // 16, length // LANES, slab_planes, comps, 16, LANES)
    return join(local, back).reshape(wavefunctions.shape)


def solution(mesh):
    placed = (
        P("band", None, "slab", None, None),
        P("slab", "band", None),
        P(None, "slab"),
        P("slab"),
        P("slab", None, None),
        P(),
    )
    return jax.shard_map(
        shards,
        mesh=mesh,
        in_specs=placed,
        out_specs=P("band", None, "slab", None, None),
        check_vma=False,
    )
```

```python
import functools

import numpy as np

import jax
import jax.numpy as jnp
from jax import lax
from jax.experimental import pallas as pl
from jax.experimental.pallas import tpu as pltpu
from jax.sharding import PartitionSpec as P

NG = 256
BOX = 12
SLAB_PLANES = 4
PAD = 16
LANES = 128
HEAP = LANES // PAD
F32 = jnp.float32
BF16 = jnp.bfloat16
HIGHEST = lax.Precision.HIGHEST
VMEM_LIMIT = 28 * 1024 * 1024
VMEM_MOST = 62 * 1024 * 1024
NT = (((1,), (1,)), ((), ()))
TN = (((0,), (0,)), ((), ()))


def kinetic_table(length):
    counter = np.arange(length)
    signed = np.where(counter < length // 2, counter, counter - length).astype(np.float64)
    angle = 2.0 * np.pi * ((counter[:, None] * counter[None, :]) % length) / length
    spectrum = signed**2 / (3.0 * (length // 2) ** 2)
    row = (np.cos(angle) * spectrum[None, :]).sum(1) / length
    table = row[(counter[:, None] - counter[None, :]) % length]
    high = jnp.asarray(table, F32).astype(BF16)
    low = (jnp.asarray(table, F32) - high.astype(F32)).astype(BF16)
    return high, low


def whole(space=pltpu.VMEM):
    return pl.BlockSpec(memory_space=space)


def dot(a, b, dims=None, precision=None):
    if dims is None:
        dims = (((1,), (0,)), ((), ()))
    return lax.dot_general(a, b, dims, precision=precision, preferred_element_type=F32)


def along_z_kernel(high_ref, low_ref, in_ref, *refs):
    out_ref, token_ref, wide, result = refs[-4:]
    token_ref[...] = jnp.zeros_like(token_ref)
    length, comps = in_ref.shape[:2]
    for c in range(comps):
        wide[c] = in_ref[:, c].astype(F32).reshape(length * 16, LANES)
        for i in range(8):
            left = wide[c, pl.ds(2 * i, length, stride=16), :]
            right = wide[c, pl.ds(2 * i + 1, length, stride=16), :]
            both = jnp.concatenate([left, right], axis=1).astype(BF16)
            out = dot(high_ref[...], both) + dot(low_ref[...], both)
            result[c, pl.ds(2 * i, length, stride=16), :] = out[:, :LANES]
            result[c, pl.ds(2 * i + 1, length, stride=16), :] = out[:, LANES:]
        out_ref[:, c] = result[c].reshape(length, 16, LANES).astype(BF16)


def along_z(high, low, block, after):
    length, comps = block.shape[:2]
    return pl.pallas_call(
        along_z_kernel,
        out_shape=(
            jax.ShapeDtypeStruct(block.shape, BF16),
            jax.ShapeDtypeStruct((8, LANES), F32),
        ),
        in_specs=[whole()] * 3 + [whole(pl.ANY)] * len(after),
        out_specs=(whole(), whole()),
        scratch_shapes=[pltpu.VMEM((comps, length * 16, LANES), F32)] * 2,
        compiler_params=pltpu.CompilerParams(vmem_limit_bytes=VMEM_LIMIT),
        cost_estimate=pl.CostEstimate(
            flops=4 * length * block.size, bytes_accessed=4 * block.size, transcendentals=0
        ),
        name="along_z",
    )(high, low, block, *after)


def select_matrix(facts, length):
    column = lax.broadcasted_iota(jnp.int32, (length, LANES), 0).astype(F32)
    return jnp.where(column == facts[0:1], 1.0, 0.0).astype(BF16)


def heap_matrix():
    lane = lax.broadcasted_iota(jnp.int32, (HEAP, LANES), 1)
    atom = lax.broadcasted_iota(jnp.int32, (HEAP, LANES), 0)
    return jnp.where(lane // PAD == atom, 1.0, 0.0).astype(F32)


def read_rows(cargo_refs, facts, rows_ref, sem, reach, stretch):
    heaps = len(cargo_refs)
    for d in range(reach):
        for r in range(heaps):
            block = cargo_refs[r][(d + 1) * stretch - PAD : (d + 1) * stretch, :].astype(F32)
            facts[d * heaps + r] = block
    rows = jnp.concatenate([facts[i, 1:2] for i in range(reach * heaps)], axis=0)
    rows_ref[0][...] = rows.astype(jnp.int32)
    copy = pltpu.make_async_copy(rows_ref[0], rows_ref[1], sem)
    copy.start()
    return copy


def read_weights(cargo_ref, at, count, weights):
    weights[0:count, :] = cargo_ref[pl.ds(pl.multiple_of(at, 16), count), :].astype(F32)


def box_weight(weights, p):
    return jnp.concatenate(
        [weights[(p * SLAB_PLANES + z) * BOX : (p * SLAB_PLANES + z) * BOX + PAD, :] for z in range(SLAB_PLANES)],
        axis=0,
    )


def project_kernel(wave_ref, *refs, heaps, reach, nproj):
    cargo_refs = refs[:heaps]
    out_ref, field, sums, weights, facts, rows_vmem, rows_smem, sem = refs[heaps:]
    planes, length = wave_ref.shape[0], wave_ref.shape[1]
    parts = planes // SLAB_PLANES
    count = nproj * SLAB_PLANES * BOX
    stretch = count + PAD
    size = SLAB_PLANES * PAD
    copy = read_rows(cargo_refs, facts, (rows_vmem, rows_smem), sem, reach, stretch)
    for i in range(planes):
        for half in range(2):
            part = wave_ref[i, :, half * LANES : (half + 1) * LANES].astype(F32)
            field[i, half, 0:length, :] = part
            field[i, half, length : length + PAD, :] = part[0:PAD]
    weights[count : count + PAD, :] = jnp.zeros((PAD, LANES), F32)
    lane = lax.broadcasted_iota(jnp.int32, (planes * PAD, LANES), 1)
    line = lax.broadcasted_iota(jnp.int32, (planes * PAD, LANES), 0)
    lane = jnp.where(line % PAD < BOX, lane // PAD, -1)
    copy.wait()

    for heap in range(heaps):

        def step(d, carry, heap=heap):
            index = d * heaps + heap
            select = select_matrix(facts[index], length)
            taken = jnp.zeros((planes * PAD, LANES), F32)
            for a in range(HEAP):
                y0 = rows_smem[index, a * PAD]
                left = field[:, 0, pl.ds(y0, PAD), :].reshape(planes * PAD, LANES)
                right = field[:, 1, pl.ds(y0, PAD), :].reshape(planes * PAD, LANES)
                window = jnp.concatenate([left, right], axis=1).astype(BF16)
                taken = jnp.where(lane == a, dot(window, select), taken)
            read_weights(cargo_refs[heap], d * stretch, count, weights)
            lines = []
            for p in range(nproj):
                weight = box_weight(weights, p)
                for part in range(parts):
                    product = weight * taken[part * size : (part + 1) * size]
                    lines.append(jnp.sum(product, axis=0, keepdims=True))
            at = pl.multiple_of(index * nproj * parts, 8)
            sums[pl.ds(at, nproj * parts), :] = jnp.concatenate(lines, axis=0)
            return carry

        lax.fori_loop(0, reach, step, 0)
    per_reach = heaps * nproj * parts
    for d in range(reach):
        out_ref[d] = dot(
            heap_matrix(), sums[d * per_reach : (d + 1) * per_reach, :], NT, HIGHEST
        )


def cargo_scratch(groups, nproj):
    return [
        pltpu.VMEM((nproj * SLAB_PLANES * BOX + PAD, LANES), F32),
        pltpu.VMEM((groups, PAD, LANES), F32),
        pltpu.VMEM((groups, LANES), jnp.int32),
        pltpu.SMEM((groups, LANES), jnp.int32),
        pltpu.SemaphoreType.DMA,
    ]


def project(wave, cargo, reach, nproj):
    heaps = len(cargo)
    planes, length, _ = wave.shape
    parts = planes // SLAB_PLANES
    return pl.pallas_call(
        functools.partial(project_kernel, heaps=heaps, reach=reach, nproj=nproj),
        out_shape=jax.ShapeDtypeStruct((reach, HEAP, heaps * nproj * parts), F32),
        in_specs=[whole()] * (1 + heaps),
        out_specs=whole(),
        scratch_shapes=[
            pltpu.VMEM((planes, 2, length + PAD, LANES), F32),
            pltpu.VMEM((reach * heaps * nproj * parts, LANES), F32),
            *cargo_scratch(reach * heaps, nproj),
        ],
        compiler_params=pltpu.CompilerParams(vmem_limit_bytes=VMEM_LIMIT),
        cost_estimate=pl.CostEstimate(
            flops=33_000_000_000, bytes_accessed=5_000_000, transcendentals=0
        ),
        name="project",
    )(wave, *cargo)


def local_kernel(where_ref, mix_ref, high_ref, low_ref, wave_ref, *refs, heaps, reach, nproj):
    cargo_refs, well_refs = refs[:heaps], refs[heaps : 2 * heaps]
    mine_ref, pair_ref, above_ref, below_ref, far_ref, _, out_ref = refs[2 * heaps : 2 * heaps + 7]
    total, spread, well, weights, facts, rows_vmem, rows_smem, sem = refs[2 * heaps + 7 :]
    planes, length = wave_ref.shape[0], wave_ref.shape[1]
    parts = planes // SLAB_PLANES
    count = nproj * SLAB_PLANES * BOX
    stretch = count + PAD
    size = SLAB_PLANES * PAD
    per_reach = heaps * nproj * parts
    share = length // heaps
    copy = read_rows(cargo_refs, facts, (rows_vmem, rows_smem), sem, reach, stretch)

    for r in range(heaps):
        place = lax.rem(where_ref[0] + r, heaps) * share
        for half in range(2):
            for z in range(SLAB_PLANES):
                at = (half * SLAB_PLANES + z) * share
                well[half, z, pl.ds(pl.multiple_of(place, 16), share), :] = well_refs[r][at : at + share, :].astype(F32)

    def fill(i, carry):
        wave = wave_ref[i]
        value = dot(wave, high_ref[...]) + dot(wave, low_ref[...])
        value += dot(high_ref[...], wave) + dot(low_ref[...], wave)
        wide = wave.astype(F32)
        for half in range(2):
            at = slice(half * LANES, (half + 1) * LANES)
            potential = well[half, lax.rem(i, SLAB_PLANES)]
            total[i, half, 0:length, :] = value[:, at] + potential * wide[:, at]
            total[i, half, length : length + PAD, :] = jnp.zeros((PAD, LANES), F32)
        return carry

    lax.fori_loop(0, planes, fill, 0)
    even = [far_ref, below_ref.at[0], below_ref.at[1], mine_ref, pair_ref.at[1], above_ref.at[0], above_ref.at[1]]
    odd = [below_ref.at[0], below_ref.at[1], pair_ref.at[0], mine_ref, above_ref.at[0], above_ref.at[1], far_ref]
    is_even = lax.rem(where_ref[1], 2) == 0
    for e in range(reach):
        full = None
        for d in range(reach):
            at = reach - 1 + d - e
            value = jnp.where(is_even, even[at][d], odd[at][d])
            full = value if full is None else full + value
        coefficients = dot(full, mix_ref[...], None, HIGHEST)
        spread[e * per_reach : (e + 1) * per_reach, :] = dot(
            coefficients, heap_matrix(), TN, HIGHEST
        )
    weights[count : count + PAD, :] = jnp.zeros((PAD, LANES), F32)
    lane = lax.broadcasted_iota(jnp.int32, (planes * PAD, LANES), 1)
    line = lax.broadcasted_iota(jnp.int32, (planes * PAD, LANES), 0)
    lane = jnp.where(line % PAD < BOX, lane // PAD, -1)
    copy.wait()

    for heap in range(heaps):

        def step(d, carry, heap=heap):
            index = d * heaps + heap
            select = select_matrix(facts[index], length)
            at = pl.multiple_of(index * nproj * parts, 8)
            lines = spread[pl.ds(at, nproj * parts), :] * facts[index, 2:3]
            read_weights(cargo_refs[heap], d * stretch, count, weights)
            blocks = [jnp.zeros((size, LANES), F32) for _ in range(parts)]
            for p in range(nproj):
                weight = box_weight(weights, p)
                for part in range(parts):
                    at = p * parts + part
                    blocks[part] = blocks[part] + weight * lines[at : at + 1, :]
            blocks = jnp.concatenate(blocks, axis=0)
            for a in range(HEAP):
                y0 = rows_smem[index, a * PAD]
                one = jnp.where(lane == a, blocks, 0.0).astype(BF16)
                placed = dot(one, select, NT)
                for half in range(2):
                    part = placed[:, half * LANES : (half + 1) * LANES]
                    total[:, half, pl.ds(y0, PAD), :] += part.reshape(planes, PAD, LANES)
            return carry

        lax.fori_loop(0, reach, step, 0)

    def finish(i, carry):
        for half in range(2):
            at = slice(half * LANES, (half + 1) * LANES)
            first = total[i, half, 0:PAD, :] + total[i, half, length : length + PAD, :]
            out_ref[i, 0:PAD, at] = first.astype(BF16)
            out_ref[i, PAD:length, at] = total[i, half, PAD:length, :].astype(BF16)
        return carry

    lax.fori_loop(0, planes, finish, 0)


def local_part(where, mix, high, low, wave, cargo, wells, exchanged, after, nproj):
    heaps = len(cargo)
    planes, length, _ = wave.shape
    parts = planes // SLAB_PLANES
    reach = exchanged[0].shape[0]
    return pl.pallas_call(
        functools.partial(local_kernel, heaps=heaps, reach=reach, nproj=nproj),
        out_shape=jax.ShapeDtypeStruct(wave.shape, BF16),
        in_specs=[whole(pltpu.SMEM)] + [whole()] * (4 + 2 * heaps + len(exchanged)) + [whole(pl.ANY)],
        out_specs=whole(),
        scratch_shapes=[
            pltpu.VMEM((planes, 2, length + PAD, LANES), F32),
            pltpu.VMEM((reach * heaps * nproj * parts, LANES), F32),
            pltpu.VMEM((2, SLAB_PLANES, length, LANES), F32),
            *cargo_scratch(reach * heaps, nproj),
        ],
        compiler_params=pltpu.CompilerParams(vmem_limit_bytes=VMEM_LIMIT),
        cost_estimate=pl.CostEstimate(
            flops=10_000_000_000, bytes_accessed=10_000_000, transcendentals=0
        ),
        name="local",
    )(where, mix, high, low, wave, *cargo, *wells, *exchanged, after)


def pack_kernel(in_ref, after_ref, out_ref):
    bands, rows, columns, slab_planes, comps = out_ref.shape[:5]
    for b in range(bands):
        for c in range(comps):
            for z in range(slab_planes):
                plane = (b * comps + c) * slab_planes + z
                for r in range(rows):
                    for h in range(columns):
                        at = (plane, slice(r * 16, (r + 1) * 16), slice(h * LANES, (h + 1) * LANES))
                        out_ref[b, r, h, z, c] = in_ref[at]


def pack(wave, bands, after):
    planes, length, _ = wave.shape
    comps = planes // SLAB_PLANES // bands
    count = 4
    row_blocks, halves = length // 16, length // LANES
    shape = (bands, row_blocks, halves, SLAB_PLANES, comps, 16, LANES)
    return pl.pallas_call(
        pack_kernel,
        out_shape=jax.ShapeDtypeStruct(shape, BF16),
        grid=(count,),
        in_specs=[
            pl.BlockSpec((planes, length // count, length), lambda i: (0, i, 0)),
            whole(pl.ANY),
        ],
        out_specs=pl.BlockSpec(
            (bands, row_blocks // count) + shape[2:], lambda i: (0, i, 0, 0, 0, 0, 0)
        ),
        compiler_params=pltpu.CompilerParams(vmem_limit_bytes=VMEM_LIMIT),
        cost_estimate=pl.CostEstimate(flops=0, bytes_accessed=4 * wave.size, transcendentals=0),
        name="pack",
    )(wave, after)


def gather_rows(nproj):
    size = SLAB_PLANES * BOX * nproj
    table = np.zeros((size, size), np.float32)
    for p in range(nproj):
        for z in range(SLAB_PLANES):
            for j in range(BOX):
                table[(p * SLAB_PLANES + z) * BOX + j, (z * BOX + j) * nproj + p] = 1.0
    return jnp.asarray(table, BF16)


def frame_kernel(where_ref, box_ref, count_ref, share_ref, order_ref, *refs):
    out_refs, dense = refs[:-1], refs[-1]
    heap = share_ref.shape[0]
    nproj, cells = share_ref.shape[1:]
    band, anchor = where_ref[0], where_ref[1] * SLAB_PLANES
    lane = lax.broadcasted_iota(jnp.int32, (nproj, LANES), 1)
    for a in range(heap):
        values = share_ref[a].astype(F32)
        tiles = [values[:, t : min(t + LANES, cells)] for t in range(0, cells, LANES)]
        gap = LANES - tiles[-1].shape[1]
        if gap:
            tiles[-1] = jnp.concatenate([tiles[-1], jnp.zeros((nproj, gap), F32)], axis=1)
        mine = (lane // PAD == a) & (lane % PAD < BOX)
        for m in range(cells // BOX):
            tile, skip = m * BOX // LANES, m * BOX % LANES
            source = tiles[tile]
            if skip + BOX > LANES:
                source = jnp.where(lane >= skip, source, tiles[tile + 1])
            shift = (a * PAD - skip) % LANES
            if shift:
                source = pltpu.roll(source, shift, 1)
            at = (m // BOX, slice(m % BOX * nproj, (m % BOX + 1) * nproj))
            dense[at] = jnp.where(mine, source, dense[at] if a else 0.0)

    lane = lax.broadcasted_iota(jnp.int32, (1, LANES), 1)
    offset = jnp.zeros((1, LANES), jnp.int32)
    row0 = jnp.zeros((1, LANES), jnp.int32)
    column0 = jnp.zeros((1, LANES), jnp.int32)
    live = jnp.zeros((1, LANES), F32)
    for a in range(heap):
        slot = band * heap + a
        mine = lane // PAD == a
        offset = jnp.where(mine, box_ref[0, slot] - anchor, offset)
        row0 = jnp.where(mine, box_ref[1, slot], row0)
        column0 = jnp.where(mine, box_ref[2, slot], column0)
        live = jnp.where(mine, jnp.where(slot < count_ref[0], 1.0, 0.0), live)
    k = lane % PAD
    target = jnp.where(k < BOX, (column0 + k) % NG, -1)
    facts = jnp.concatenate(
        [target.astype(F32), row0.astype(F32), live, jnp.zeros((PAD - 3, LANES), F32)], axis=0
    ).astype(BF16)

    rows = nproj * SLAB_PLANES * BOX
    for d in range(len(out_refs)):
        planes = []
        for z in range(SLAB_PLANES):
            f = d * SLAB_PLANES + z
            framed = jnp.zeros((BOX * nproj, LANES), F32)
            for o in range(SLAB_PLANES):
                if 0 <= f - o < BOX:
                    framed = jnp.where(offset == o, dense[f - o], framed)
            planes.append(framed)
        planes = jnp.concatenate(planes, axis=0).astype(BF16)
        out_refs[d][0:rows, :] = dot(order_ref[...], planes).astype(BF16)
        out_refs[d][rows : rows + PAD, :] = facts


def frame(where, projectors, atom_box, atom_count):
    _, nproj, cells = projectors.shape
    reach = (BOX + SLAB_PLANES) // SLAB_PLANES
    order = gather_rows(nproj)
    shape = (nproj * SLAB_PLANES * BOX + PAD, LANES)
    return pl.pallas_call(
        frame_kernel,
        out_shape=(jax.ShapeDtypeStruct(shape, BF16),) * reach,
        grid_spec=pltpu.PrefetchScalarGridSpec(
            num_scalar_prefetch=3,
            grid=(1,),
            in_specs=[
                pl.BlockSpec((HEAP, nproj, cells), lambda i, where, box, count: (where[0], 0, 0)),
                whole(),
            ],
            out_specs=(pl.BlockSpec(shape, lambda i, where, box, count: (0, 0)),) * reach,
            scratch_shapes=[pltpu.VMEM((BOX, nproj * BOX, LANES), F32)],
        ),
        compiler_params=pltpu.CompilerParams(vmem_limit_bytes=VMEM_MOST),
        cost_estimate=pl.CostEstimate(
            flops=1_000_000_000, bytes_accessed=1_000_000, transcendentals=0
        ),
        name="frame",
    )(where, atom_box, atom_count, projectors, order)


def join_kernel(local_ref, arrived_ref, out_ref, near, here, there, near_sem, in_sem, out_sem):
    bands, rows, columns, slab_planes, comps = arrived_ref.shape[:5]
    count = in_sem.shape[0]
    step = rows // count
    loads, stores = [], []
    for i in range(count):
        at = slice(i * step, (i + 1) * step)
        lines = slice(i * step * 16, (i + 1) * step * 16)
        loads.append(pltpu.make_async_copy(local_ref.at[:, lines], near.at[:, lines], near_sem.at[i]))
        loads.append(pltpu.make_async_copy(arrived_ref.at[:, at], here.at[:, at], in_sem.at[i]))
        stores.append(pltpu.make_async_copy(there.at[:, lines], out_ref.at[:, lines], out_sem.at[i]))
    for load in loads:
        load.start()
    for i in range(count):
        loads[2 * i].wait()
        loads[2 * i + 1].wait()
        for r in range(i * step, (i + 1) * step):
            for b in range(bands):
                for c in range(comps):
                    for z in range(slab_planes):
                        plane = (b * comps + c) * slab_planes + z
                        for h in range(columns):
                            at = (plane, slice(r * 16, (r + 1) * 16), slice(h * LANES, (h + 1) * LANES))
                            value = near[at].astype(F32) + here[b, r, h, z, c].astype(F32)
                            there[at] = value.astype(BF16)
        stores[i].start()
    for store in stores:
        store.wait()


def join(local, arrived):
    count = 8
    return pl.pallas_call(
        join_kernel,
        out_shape=jax.ShapeDtypeStruct(local.shape, BF16),
        in_specs=[whole(pltpu.HBM), whole(pltpu.HBM)],
        out_specs=whole(pltpu.HBM),
        scratch_shapes=[
            pltpu.VMEM(local.shape, BF16),
            pltpu.VMEM(arrived.shape, BF16),
            pltpu.VMEM(local.shape, BF16),
            pltpu.SemaphoreType.DMA((count,)),
            pltpu.SemaphoreType.DMA((count,)),
            pltpu.SemaphoreType.DMA((count,)),
        ],
        compiler_params=pltpu.CompilerParams(vmem_limit_bytes=VMEM_MOST),
        cost_estimate=pl.CostEstimate(
            flops=2 * local.size, bytes_accessed=6 * local.size, transcendentals=0
        ),
        name="join",
    )(local, arrived)


def ahead(block, distance, axis="slab"):
    size = lax.axis_size(axis)
    return lax.ppermute(block, axis, [(i, (i + distance) % size) for i in range(size)])


def shards(wavefunctions, potential, atom_box, atom_count, projectors, coupling):
    bands, comps, slab_planes, length, _ = wavefunctions.shape
    parts = bands * comps
    planes = parts * slab_planes
    slabs = lax.axis_size("slab")
    heaps = lax.axis_size("band")
    nproj = projectors.shape[1]
    high, low = kinetic_table(length)
    wave = wavefunctions.reshape(planes, length, length)

    where = jnp.stack([lax.axis_index("band"), lax.axis_index("slab")]).astype(jnp.int32)
    framed = frame(where, projectors, atom_box, atom_count)
    reach = len(framed)
    arrived = [framed[0]] + [ahead(framed[d], d) for d in range(1, reach)]

    send = pack(wave, bands, arrived[1]).reshape(slabs, slab_planes * comps, 16, LANES)
    columns = lax.all_to_all(send, "slab", split_axis=0, concat_axis=0, tiled=True)

    cargo = jnp.concatenate(arrived, axis=0)
    cargo = [cargo] + [ahead(cargo, -r, "band") for r in range(1, heaps)]
    well = potential.astype(BF16).reshape(slab_planes, length // heaps, 2, LANES)
    well = well.transpose(2, 0, 1, 3).reshape(-1, LANES)
    wells = [well] + [ahead(well, -r, "band") for r in range(1, heaps)]

    partial = project(wave, cargo, reach, nproj)
    other = lax.ppermute(partial, "slab", [(i, i ^ 1) for i in range(slabs)])
    even = where[1] % 2 == 0
    pair = jnp.stack([jnp.where(even, partial, other), jnp.where(even, other, partial)])
    above = ahead(pair, -2)
    below = ahead(pair, 2)
    far = lax.ppermute(
        partial, "slab", [(i, (i + 3 if i % 2 else i - 3) % slabs) for i in range(slabs)]
    )

    symmetric = (coupling + coupling.T) * 0.5
    mix = jnp.einsum(
        "gh,pq,bc->gqbhpc", jnp.eye(heaps, dtype=F32), symmetric, jnp.eye(parts, dtype=F32),
        precision=HIGHEST,
    ).reshape(heaps * nproj * parts, heaps * nproj * parts)

    exchanged = [partial, pair, above, below, far]
    columns, token = along_z(high, low, columns.reshape(length, comps, 16, LANES), exchanged[2:])
    local = local_part(where, mix, high, low, wave, cargo, wells, exchanged, token, nproj)
    columns = columns.reshape(slabs, slab_planes * comps, 16, LANES)
    back = lax.all_to_all(columns, "slab", split_axis=0, concat_axis=0, tiled=True)
    back = back.reshape(bands, length // 16, length // LANES, slab_planes, comps, 16, LANES)
    return join(local, back).reshape(wavefunctions.shape)


def solution(mesh):
    placed = (
        P("band", None, "slab", None, None),
        P("slab", "band", None),
        P(None, "slab"),
        P("slab"),
        P("slab", None, None),
        P(),
    )
    return jax.shard_map(
        shards,
        mesh=mesh,
        in_specs=placed,
        out_specs=P("band", None, "slab", None, None),
        check_vma=False,
    )
```

```python
import functools

import numpy as np

import jax
import jax.numpy as jnp
from jax import lax
from jax.experimental import pallas as pl
from jax.experimental.pallas import tpu as pltpu
from jax.sharding import PartitionSpec as P

NG = 256
BOX = 12
SLAB_PLANES = 4
PAD = 16
PITCH = 20
LANES = 128
HEAP = LANES // PAD
F32 = jnp.float32
BF16 = jnp.bfloat16
HIGHEST = lax.Precision.HIGHEST
VMEM_LIMIT = 28 * 1024 * 1024
VMEM_MOST = 62 * 1024 * 1024
NT = (((1,), (1,)), ((), ()))
TN = (((0,), (0,)), ((), ()))


def kinetic_table(length):
    counter = np.arange(length)
    signed = np.where(counter < length // 2, counter, counter - length).astype(np.float64)
    angle = 2.0 * np.pi * ((counter[:, None] * counter[None, :]) % length) / length
    spectrum = signed**2 / (3.0 * (length // 2) ** 2)
    row = (np.cos(angle) * spectrum[None, :]).sum(1) / length
    table = row[(counter[:, None] - counter[None, :]) % length]
    high = jnp.asarray(table, F32).astype(BF16)
    low = (jnp.asarray(table, F32) - high.astype(F32)).astype(BF16)
    return jnp.stack([high, low])


def whole(space=pltpu.VMEM):
    return pl.BlockSpec(memory_space=space)


def dot(a, b, dims=None, precision=None):
    if dims is None:
        dims = (((1,), (0,)), ((), ()))
    return lax.dot_general(a, b, dims, precision=precision, preferred_element_type=F32)


def along_z_kernel(table_ref, in_ref, *refs):
    out_ref, token_ref, wide, result = refs[-4:]
    token_ref[...] = jnp.zeros_like(token_ref)
    length, comps, rows = in_ref.shape[:3]
    for c in range(comps):
        for z in range(length):
            wide[c, z * PITCH : z * PITCH + rows, :] = in_ref[z, c].astype(F32)
        for i in range(rows // 2):
            left = wide[c, pl.ds(2 * i, length, stride=PITCH), :]
            right = wide[c, pl.ds(2 * i + 1, length, stride=PITCH), :]
            both = jnp.concatenate([left, right], axis=1).astype(BF16)
            out = dot(table_ref[0], both) + dot(table_ref[1], both)
            result[c, pl.ds(2 * i, length, stride=PITCH), :] = out[:, :LANES]
            result[c, pl.ds(2 * i + 1, length, stride=PITCH), :] = out[:, LANES:]
        for z in range(length):
            out_ref[z, c] = result[c, z * PITCH : z * PITCH + rows, :].astype(BF16)


def along_z(table, block, after):
    length, comps = block.shape[:2]
    return pl.pallas_call(
        along_z_kernel,
        out_shape=(
            jax.ShapeDtypeStruct(block.shape, BF16),
            jax.ShapeDtypeStruct((8, LANES), F32),
        ),
        in_specs=[whole()] * 2 + [whole(pl.ANY)] * len(after),
        out_specs=(whole(), whole()),
        scratch_shapes=[pltpu.VMEM((comps, length * PITCH, LANES), F32)] * 2,
        compiler_params=pltpu.CompilerParams(vmem_limit_bytes=VMEM_LIMIT),
        cost_estimate=pl.CostEstimate(
            flops=4 * length * block.size, bytes_accessed=4 * block.size, transcendentals=0
        ),
        name="along_z",
    )(table, block, *after)


def select_matrix(facts, length):
    column = lax.broadcasted_iota(jnp.int32, (length, LANES), 0).astype(F32)
    return jnp.where(column == facts[0:1], 1.0, 0.0).astype(BF16)


def heap_matrix():
    lane = lax.broadcasted_iota(jnp.int32, (HEAP, LANES), 1)
    atom = lax.broadcasted_iota(jnp.int32, (HEAP, LANES), 0)
    return jnp.where(lane // PAD == atom, 1.0, 0.0).astype(F32)


def read_rows(cargo_refs, facts, rows_ref, sem, reach, stretch):
    heaps = len(cargo_refs)
    for d in range(reach):
        for r in range(heaps):
            block = cargo_refs[r][(d + 1) * stretch - PAD : (d + 1) * stretch, :].astype(F32)
            facts[d * heaps + r] = block
    rows = jnp.concatenate([facts[i, 1:2] for i in range(reach * heaps)], axis=0)
    rows_ref[0][...] = rows.astype(jnp.int32)
    copy = pltpu.make_async_copy(rows_ref[0], rows_ref[1], sem)
    copy.start()
    return copy


def read_weights(cargo_ref, at, count, weights):
    weights[0:count, :] = cargo_ref[pl.ds(pl.multiple_of(at, 16), count), :].astype(F32)


def box_weight(weights, p):
    return jnp.concatenate(
        [weights[(p * SLAB_PLANES + z) * BOX : (p * SLAB_PLANES + z) * BOX + PAD, :] for z in range(SLAB_PLANES)],
        axis=0,
    )


def project_kernel(wave_ref, *refs, heaps, reach, nproj):
    cargo_refs = refs[:heaps]
    out_ref, field, sums, weights, facts, rows_vmem, rows_smem, sem = refs[heaps:]
    planes, length = wave_ref.shape[0], wave_ref.shape[1]
    parts = planes // SLAB_PLANES
    count = nproj * SLAB_PLANES * BOX
    stretch = count + PAD
    size = SLAB_PLANES * PAD
    copy = read_rows(cargo_refs, facts, (rows_vmem, rows_smem), sem, reach, stretch)
    for i in range(planes):
        for half in range(2):
            part = wave_ref[i, :, half * LANES : (half + 1) * LANES].astype(F32)
            field[i, half, 0:length, :] = part
            field[i, half, length : length + PAD, :] = part[0:PAD]
    weights[count : count + PAD, :] = jnp.zeros((PAD, LANES), F32)
    lane = lax.broadcasted_iota(jnp.int32, (planes * PAD, LANES), 1)
    line = lax.broadcasted_iota(jnp.int32, (planes * PAD, LANES), 0)
    lane = jnp.where(line % PAD < BOX, lane // PAD, -1)
    copy.wait()

    for heap in range(heaps):

        def step(d, carry, heap=heap):
            index = d * heaps + heap
            select = select_matrix(facts[index], length)
            taken = jnp.zeros((planes * PAD, LANES), F32)
            for a in range(HEAP):
                y0 = rows_smem[index, a * PAD]
                left = field[:, 0, pl.ds(y0, PAD), :].reshape(planes * PAD, LANES)
                right = field[:, 1, pl.ds(y0, PAD), :].reshape(planes * PAD, LANES)
                window = jnp.concatenate([left, right], axis=1).astype(BF16)
                taken = jnp.where(lane == a, dot(window, select), taken)
            read_weights(cargo_refs[heap], d * stretch, count, weights)
            lines = []
            for p in range(nproj):
                weight = box_weight(weights, p)
                for part in range(parts):
                    product = weight * taken[part * size : (part + 1) * size]
                    lines.append(jnp.sum(product, axis=0, keepdims=True))
            at = pl.multiple_of(index * nproj * parts, 8)
            sums[pl.ds(at, nproj * parts), :] = jnp.concatenate(lines, axis=0)
            return carry

        lax.fori_loop(0, reach, step, 0)
    per_reach = heaps * nproj * parts
    for d in range(reach):
        out_ref[d] = dot(
            heap_matrix(), sums[d * per_reach : (d + 1) * per_reach, :], NT, HIGHEST
        )


def cargo_scratch(groups, nproj):
    return [
        pltpu.VMEM((nproj * SLAB_PLANES * BOX + PAD, LANES), F32),
        pltpu.VMEM((groups, PAD, LANES), F32),
        pltpu.VMEM((groups, LANES), jnp.int32),
        pltpu.SMEM((groups, LANES), jnp.int32),
        pltpu.SemaphoreType.DMA,
    ]


def project(wave, cargo, reach, nproj):
    heaps = len(cargo)
    planes, length, _ = wave.shape
    parts = planes // SLAB_PLANES
    return pl.pallas_call(
        functools.partial(project_kernel, heaps=heaps, reach=reach, nproj=nproj),
        out_shape=jax.ShapeDtypeStruct((reach, HEAP, heaps * nproj * parts), F32),
        in_specs=[whole()] * (1 + heaps),
        out_specs=whole(),
        scratch_shapes=[
            pltpu.VMEM((planes, 2, length + PAD, LANES), F32),
            pltpu.VMEM((reach * heaps * nproj * parts, LANES), F32),
            *cargo_scratch(reach * heaps, nproj),
        ],
        compiler_params=pltpu.CompilerParams(vmem_limit_bytes=VMEM_LIMIT),
        cost_estimate=pl.CostEstimate(
            flops=33_000_000_000, bytes_accessed=5_000_000, transcendentals=0
        ),
        name="project",
    )(wave, *cargo)


def local_kernel(mix_ref, table_ref, wave_ref, *refs, heaps, reach, nproj):
    cargo_refs, well_refs = refs[:heaps], refs[heaps : 2 * heaps]
    mine_ref, pair_ref, above_ref, below_ref, far_ref, _, out_ref = refs[2 * heaps : 2 * heaps + 7]
    total, spread, well, weights, facts, rows_vmem, rows_smem, sem = refs[2 * heaps + 7 :]
    planes, length = wave_ref.shape[0], wave_ref.shape[1]
    parts = planes // SLAB_PLANES
    count = nproj * SLAB_PLANES * BOX
    stretch = count + PAD
    size = SLAB_PLANES * PAD
    per_reach = heaps * nproj * parts
    share = length // heaps
    copy = read_rows(cargo_refs, facts, (rows_vmem, rows_smem), sem, reach, stretch)

    for r in range(heaps):
        place = lax.rem(lax.axis_index("band") + r, heaps) * share
        for half in range(2):
            for z in range(SLAB_PLANES):
                at = (half * SLAB_PLANES + z) * share
                well[half, z, pl.ds(pl.multiple_of(place, 16), share), :] = well_refs[r][at : at + share, :].astype(F32)

    def fill(i, carry):
        wave = wave_ref[i]
        value = dot(wave, table_ref[0]) + dot(wave, table_ref[1])
        value += dot(table_ref[0], wave) + dot(table_ref[1], wave)
        wide = wave.astype(F32)
        for half in range(2):
            at = slice(half * LANES, (half + 1) * LANES)
            potential = well[half, lax.rem(i, SLAB_PLANES)]
            total[i, half, 0:length, :] = value[:, at] + potential * wide[:, at]
            total[i, half, length : length + PAD, :] = jnp.zeros((PAD, LANES), F32)
        return carry

    lax.fori_loop(0, planes, fill, 0)
    even = [far_ref, below_ref.at[0], below_ref.at[1], mine_ref, pair_ref.at[1], above_ref.at[0], above_ref.at[1]]
    odd = [below_ref.at[0], below_ref.at[1], pair_ref.at[0], mine_ref, above_ref.at[0], above_ref.at[1], far_ref]
    is_even = lax.rem(lax.axis_index("slab"), 2) == 0
    for e in range(reach):
        full = None
        for d in range(reach):
            at = reach - 1 + d - e
            value = jnp.where(is_even, even[at][d], odd[at][d])
            full = value if full is None else full + value
        coefficients = dot(full, mix_ref[...], None, HIGHEST)
        spread[e * per_reach : (e + 1) * per_reach, :] = dot(
            coefficients, heap_matrix(), TN, HIGHEST
        )
    weights[count : count + PAD, :] = jnp.zeros((PAD, LANES), F32)
    lane = lax.broadcasted_iota(jnp.int32, (planes * PAD, LANES), 1)
    line = lax.broadcasted_iota(jnp.int32, (planes * PAD, LANES), 0)
    lane = jnp.where(line % PAD < BOX, lane // PAD, -1)
    copy.wait()

    for heap in range(heaps):

        def step(d, carry, heap=heap):
            index = d * heaps + heap
            select = select_matrix(facts[index], length)
            at = pl.multiple_of(index * nproj * parts, 8)
            lines = spread[pl.ds(at, nproj * parts), :] * facts[index, 2:3]
            read_weights(cargo_refs[heap], d * stretch, count, weights)
            blocks = [jnp.zeros((size, LANES), F32) for _ in range(parts)]
            for p in range(nproj):
                weight = box_weight(weights, p)
                for part in range(parts):
                    at = p * parts + part
                    blocks[part] = blocks[part] + weight * lines[at : at + 1, :]
            blocks = jnp.concatenate(blocks, axis=0)
            for a in range(HEAP):
                y0 = rows_smem[index, a * PAD]
                one = jnp.where(lane == a, blocks, 0.0).astype(BF16)
                placed = dot(one, select, NT)
                for half in range(2):
                    part = placed[:, half * LANES : (half + 1) * LANES]
                    total[:, half, pl.ds(y0, PAD), :] += part.reshape(planes, PAD, LANES)
            return carry

        lax.fori_loop(0, reach, step, 0)

    def finish(i, carry):
        for half in range(2):
            at = slice(half * LANES, (half + 1) * LANES)
            first = total[i, half, 0:PAD, :] + total[i, half, length : length + PAD, :]
            out_ref[i, 0:PAD, at] = first.astype(BF16)
            out_ref[i, PAD:length, at] = total[i, half, PAD:length, :].astype(BF16)
        return carry

    lax.fori_loop(0, planes, finish, 0)


def local_part(mix, table, wave, cargo, wells, exchanged, after, nproj):
    heaps = len(cargo)
    planes, length, _ = wave.shape
    parts = planes // SLAB_PLANES
    reach = exchanged[0].shape[0]
    return pl.pallas_call(
        functools.partial(local_kernel, heaps=heaps, reach=reach, nproj=nproj),
        out_shape=jax.ShapeDtypeStruct(wave.shape, BF16),
        in_specs=[whole()] * (3 + 2 * heaps + len(exchanged)) + [whole(pl.ANY)],
        out_specs=whole(),
        scratch_shapes=[
            pltpu.VMEM((planes, 2, length + PAD, LANES), F32),
            pltpu.VMEM((reach * heaps * nproj * parts, LANES), F32),
            pltpu.VMEM((2, SLAB_PLANES, length, LANES), F32),
            *cargo_scratch(reach * heaps, nproj),
        ],
        compiler_params=pltpu.CompilerParams(vmem_limit_bytes=VMEM_LIMIT),
        cost_estimate=pl.CostEstimate(
            flops=10_000_000_000, bytes_accessed=10_000_000, transcendentals=0
        ),
        name="local",
    )(mix, table, wave, *cargo, *wells, *exchanged, after)


def gather_rows(nproj):
    size = SLAB_PLANES * BOX * nproj
    table = np.zeros((size, size), np.float32)
    for p in range(nproj):
        for z in range(SLAB_PLANES):
            for j in range(BOX):
                table[(p * SLAB_PLANES + z) * BOX + j, (z * BOX + j) * nproj + p] = 1.0
    return jnp.asarray(table, BF16)


def frame_kernel(
    box_ref, count_ref, projectors_ref, order_ref, wave_ref, send_ref, *refs
):
    out_refs, scratch = refs[:-10], refs[-10:]
    dense, share_ref, order, done, field, packed, fetch_sem, in_sem, out_sem, done_sem = scratch
    bands, row_blocks, columns, slab_planes, comps = packed.shape[:5]
    heap, nproj, cells = share_ref.shape
    band, anchor = lax.axis_index("band"), lax.axis_index("slab") * SLAB_PLANES
    fetch = pltpu.make_async_copy(
        projectors_ref.at[pl.ds(band * heap, heap)], share_ref, fetch_sem.at[0]
    )
    fetch.start()
    fetch_order = pltpu.make_async_copy(order_ref, order, fetch_sem.at[1])
    count = in_sem.shape[0]
    step = row_blocks // count
    loads, stores = [], []
    for i in range(count):
        lines = slice(i * step * 16, (i + 1) * step * 16)
        at = slice(i * step, (i + 1) * step)
        loads.append(pltpu.make_async_copy(wave_ref.at[:, lines], field.at[:, lines], in_sem.at[i]))
        stores.append(pltpu.make_async_copy(packed.at[:, at], send_ref.at[:, at], out_sem.at[i]))
        loads[i].start()
    fetch_order.start()
    fetch.wait()

    lane = lax.broadcasted_iota(jnp.int32, (nproj, LANES), 1)
    for a in range(heap):
        values = share_ref[a].astype(F32)
        tiles = [values[:, t : min(t + LANES, cells)] for t in range(0, cells, LANES)]
        gap = LANES - tiles[-1].shape[1]
        if gap:
            tiles[-1] = jnp.concatenate([tiles[-1], jnp.zeros((nproj, gap), F32)], axis=1)
        mine = (lane // PAD == a) & (lane % PAD < BOX)
        for m in range(cells // BOX):
            tile, skip = m * BOX // LANES, m * BOX % LANES
            source = tiles[tile]
            if skip + BOX > LANES:
                source = jnp.where(lane >= skip, source, tiles[tile + 1])
            shift = (a * PAD - skip) % LANES
            if shift:
                source = pltpu.roll(source, shift, 1)
            at = (m // BOX, slice(m % BOX * nproj, (m % BOX + 1) * nproj))
            dense[at] = jnp.where(mine, source, dense[at] if a else 0.0)

    for i in range(count):
        loads[i].wait()
        for r in range(i * step, (i + 1) * step):
            for b in range(bands):
                for c in range(comps):
                    for z in range(slab_planes):
                        plane = (b * comps + c) * slab_planes + z
                        for h in range(columns):
                            packed[b, r, h, z, c] = field[
                                plane, r * 16 : (r + 1) * 16, h * LANES : (h + 1) * LANES
                            ]
        stores[i].start()

    lane = lax.broadcasted_iota(jnp.int32, (1, LANES), 1)
    offset = jnp.zeros((1, LANES), jnp.int32)
    row0 = jnp.zeros((1, LANES), jnp.int32)
    column0 = jnp.zeros((1, LANES), jnp.int32)
    live = jnp.zeros((1, LANES), F32)
    for a in range(heap):
        slot = band * heap + a
        mine = lane // PAD == a
        offset = jnp.where(mine, box_ref[0, slot] - anchor, offset)
        row0 = jnp.where(mine, box_ref[1, slot], row0)
        column0 = jnp.where(mine, box_ref[2, slot], column0)
        live = jnp.where(mine, jnp.where(slot < count_ref[0], 1.0, 0.0), live)
    k = lane % PAD
    target = jnp.where(k < BOX, (column0 + k) % NG, -1)
    facts = jnp.concatenate(
        [target.astype(F32), row0.astype(F32), live, jnp.zeros((PAD - 3, LANES), F32)], axis=0
    ).astype(BF16)

    rows = nproj * SLAB_PLANES * BOX
    fetch_order.wait()
    for d in range(len(out_refs)):
        planes = []
        for z in range(SLAB_PLANES):
            f = d * SLAB_PLANES + z
            framed = jnp.zeros((BOX * nproj, LANES), F32)
            for o in range(SLAB_PLANES):
                if 0 <= f - o < BOX:
                    framed = jnp.where(offset == o, dense[f - o], framed)
            planes.append(framed)
        planes = jnp.concatenate(planes, axis=0).astype(BF16)
        done[d, 0:rows, :] = dot(order[...], planes).astype(BF16)
        done[d, rows : rows + PAD, :] = facts
        stores.append(
            pltpu.make_async_copy(done.at[d], out_refs[d].at[0 : rows + PAD], done_sem.at[d])
        )
        stores[-1].start()
    for store in stores:
        store.wait()


def frame(projectors, atom_box, atom_count, wave, bands):
    _, nproj, cells = projectors.shape
    planes, length, _ = wave.shape
    comps = planes // SLAB_PLANES // bands
    reach = (BOX + SLAB_PLANES) // SLAB_PLANES
    order = gather_rows(nproj)
    rows = nproj * SLAB_PLANES * BOX + PAD
    shape = jax.ShapeDtypeStruct((rows, LANES), BF16)
    send = (bands, length // 16, length // LANES, SLAB_PLANES, comps, 16, LANES)
    count = 4
    return pl.pallas_call(
        frame_kernel,
        out_shape=(
            jax.ShapeDtypeStruct(send, BF16),
            jax.ShapeDtypeStruct((reach * rows, LANES), BF16),
        )
        + (shape,) * (reach - 1),
        in_specs=[whole(pltpu.SMEM)] * 2 + [whole(pltpu.HBM)] * 3,
        out_specs=(whole(pltpu.HBM),) * (1 + reach),
        scratch_shapes=[
            pltpu.VMEM((BOX, nproj * BOX, LANES), F32),
            pltpu.VMEM((HEAP, nproj, cells), BF16),
            pltpu.VMEM(order.shape, BF16),
            pltpu.VMEM((reach, rows, LANES), BF16),
            pltpu.VMEM(wave.shape, BF16),
            pltpu.VMEM(send, BF16),
            pltpu.SemaphoreType.DMA((2,)),
            pltpu.SemaphoreType.DMA((count,)),
            pltpu.SemaphoreType.DMA((count,)),
            pltpu.SemaphoreType.DMA((reach,)),
        ],
        compiler_params=pltpu.CompilerParams(vmem_limit_bytes=VMEM_MOST),
        cost_estimate=pl.CostEstimate(
            flops=1_000_000_000, bytes_accessed=9_000_000, transcendentals=0
        ),
        name="frame",
    )(atom_box, atom_count, projectors, order, wave)


def gate_kernel(*refs):
    pass


def gate(block, after):
    return pl.pallas_call(
        gate_kernel,
        out_shape=jax.ShapeDtypeStruct(block.shape, block.dtype),
        in_specs=[whole(pltpu.HBM)] + [whole(pl.ANY)] * len(after),
        out_specs=whole(pltpu.HBM),
        input_output_aliases={0: 0},
        compiler_params=pltpu.CompilerParams(vmem_limit_bytes=VMEM_MOST),
        name="gate",
    )(block, *after)


def join_kernel(local_ref, arrived_ref, out_ref, near, here, there, near_sem, in_sem, out_sem):
    bands, rows, columns, slab_planes, comps = arrived_ref.shape[:5]
    count = in_sem.shape[0]
    step = rows // count
    loads, stores = [], []
    for i in range(count):
        at = slice(i * step, (i + 1) * step)
        lines = slice(i * step * 16, (i + 1) * step * 16)
        loads.append(pltpu.make_async_copy(local_ref.at[:, lines], near.at[:, lines], near_sem.at[i]))
        loads.append(pltpu.make_async_copy(arrived_ref.at[:, at], here.at[:, at], in_sem.at[i]))
        stores.append(pltpu.make_async_copy(there.at[:, lines], out_ref.at[:, lines], out_sem.at[i]))
    for load in loads:
        load.start()
    for i in range(count):
        loads[2 * i].wait()
        loads[2 * i + 1].wait()
        for r in range(i * step, (i + 1) * step):
            for b in range(bands):
                for c in range(comps):
                    for z in range(slab_planes):
                        plane = (b * comps + c) * slab_planes + z
                        for h in range(columns):
                            at = (plane, slice(r * 16, (r + 1) * 16), slice(h * LANES, (h + 1) * LANES))
                            value = near[at].astype(F32) + here[b, r, h, z, c].astype(F32)
                            there[at] = value.astype(BF16)
        stores[i].start()
    for store in stores:
        store.wait()


def join(local, arrived):
    count = 8
    return pl.pallas_call(
        join_kernel,
        out_shape=jax.ShapeDtypeStruct(local.shape, BF16),
        in_specs=[whole(pltpu.HBM), whole(pltpu.HBM)],
        out_specs=whole(pltpu.HBM),
        scratch_shapes=[
            pltpu.VMEM(local.shape, BF16),
            pltpu.VMEM(arrived.shape, BF16),
            pltpu.VMEM(local.shape, BF16),
            pltpu.SemaphoreType.DMA((count,)),
            pltpu.SemaphoreType.DMA((count,)),
            pltpu.SemaphoreType.DMA((count,)),
        ],
        compiler_params=pltpu.CompilerParams(vmem_limit_bytes=VMEM_MOST),
        cost_estimate=pl.CostEstimate(
            flops=2 * local.size, bytes_accessed=6 * local.size, transcendentals=0
        ),
        name="join",
    )(local, arrived)


def ahead(block, distance, axis="slab"):
    size = lax.axis_size(axis)
    return lax.ppermute(block, axis, [(i, (i + distance) % size) for i in range(size)])


def shards(wavefunctions, potential, atom_box, atom_count, projectors, coupling):
    bands, comps, slab_planes, length, _ = wavefunctions.shape
    parts = bands * comps
    planes = parts * slab_planes
    slabs = lax.axis_size("slab")
    heaps = lax.axis_size("band")
    nproj = projectors.shape[1]
    table = kinetic_table(length)
    wave = wavefunctions.reshape(planes, length, length)

    send, cargo, *framed = frame(projectors, atom_box, atom_count, wave, bands)
    reach = len(framed) + 1
    arrived = [ahead(framed[d - 1], d) for d in range(1, reach)]

    send = gate(send, arrived[:1]).reshape(slabs, slab_planes * comps, 16, LANES)
    columns = lax.all_to_all(send, "slab", split_axis=0, concat_axis=0, tiled=True)

    rows = arrived[0].shape[0]
    for d in range(1, reach):
        cargo = lax.dynamic_update_slice_in_dim(cargo, arrived[d - 1], d * rows, 0)
    cargo = [cargo] + [ahead(cargo, -r, "band") for r in range(1, heaps)]
    well = potential.astype(BF16).reshape(slab_planes, length // heaps, 2, LANES)
    well = well.transpose(2, 0, 1, 3).reshape(-1, LANES)
    wells = [well] + [ahead(well, -r, "band") for r in range(1, heaps)]

    partial = project(wave, cargo, reach, nproj)
    other = lax.ppermute(partial, "slab", [(i, i ^ 1) for i in range(slabs)])
    even = lax.axis_index("slab") % 2 == 0
    pair = jnp.stack([jnp.where(even, partial, other), jnp.where(even, other, partial)])
    above = ahead(pair, -2)
    below = ahead(pair, 2)
    far = lax.ppermute(
        partial, "slab", [(i, (i + 3 if i % 2 else i - 3) % slabs) for i in range(slabs)]
    )

    symmetric = (coupling + coupling.T) * 0.5
    mix = jnp.einsum(
        "gh,pq,bc->gqbhpc", jnp.eye(heaps, dtype=F32), symmetric, jnp.eye(parts, dtype=F32),
        precision=HIGHEST,
    ).reshape(heaps * nproj * parts, heaps * nproj * parts)

    exchanged = [partial, pair, above, below, far]
    columns, token = along_z(table, columns.reshape(length, comps, 16, LANES), exchanged[2:])
    local = local_part(mix, table, wave, cargo, wells, exchanged, token, nproj)
    columns = columns.reshape(slabs, slab_planes * comps, 16, LANES)
    back = lax.all_to_all(columns, "slab", split_axis=0, concat_axis=0, tiled=True)
    back = back.reshape(bands, length // 16, length // LANES, slab_planes, comps, 16, LANES)
    return join(local, back).reshape(wavefunctions.shape)


def solution(mesh):
    placed = (
        P("band", None, "slab", None, None),
        P("slab", "band", None),
        P(None, "slab"),
        P("slab"),
        P("slab", None, None),
        P(),
    )
    return jax.shard_map(
        shards,
        mesh=mesh,
        in_specs=placed,
        out_specs=P("band", None, "slab", None, None),
        check_vma=False,
    )
```

```python
import functools

import numpy as np

import jax
import jax.numpy as jnp
from jax import lax
from jax.experimental import pallas as pl
from jax.experimental.pallas import tpu as pltpu
from jax.sharding import PartitionSpec as P

NG = 256
BOX = 12
SLAB_PLANES = 4
PAD = 16
PITCH = 20
LANES = 128
HEAP = LANES // PAD
F32 = jnp.float32
BF16 = jnp.bfloat16
HIGHEST = lax.Precision.HIGHEST
VMEM_LIMIT = 28 * 1024 * 1024
VMEM_MOST = 62 * 1024 * 1024
NT = (((1,), (1,)), ((), ()))
TN = (((0,), (0,)), ((), ()))


def kinetic_table(length):
    counter = np.arange(length)
    signed = np.where(counter < length // 2, counter, counter - length).astype(np.float64)
    angle = 2.0 * np.pi * ((counter[:, None] * counter[None, :]) % length) / length
    spectrum = signed**2 / (3.0 * (length // 2) ** 2)
    row = (np.cos(angle) * spectrum[None, :]).sum(1) / length
    table = row[(counter[:, None] - counter[None, :]) % length]
    high = jnp.asarray(table, F32).astype(BF16)
    low = (jnp.asarray(table, F32) - high.astype(F32)).astype(BF16)
    return jnp.stack([high, low])


def whole(space=pltpu.VMEM):
    return pl.BlockSpec(memory_space=space)


def dot(a, b, dims=None, precision=None):
    if dims is None:
        dims = (((1,), (0,)), ((), ()))
    return lax.dot_general(a, b, dims, precision=precision, preferred_element_type=F32)


def along_z_kernel(table_ref, in_ref, *refs):
    out_ref, token_ref, wide, result = refs[-4:]
    token_ref[...] = jnp.zeros_like(token_ref)
    length, comps, rows = in_ref.shape[:3]
    for c in range(comps):
        for z in range(length):
            wide[c, z * PITCH : z * PITCH + rows, :] = in_ref[z, c].astype(F32)
        for i in range(rows // 2):
            left = wide[c, pl.ds(2 * i, length, stride=PITCH), :]
            right = wide[c, pl.ds(2 * i + 1, length, stride=PITCH), :]
            both = jnp.concatenate([left, right], axis=1).astype(BF16)
            out = dot(table_ref[0], both) + dot(table_ref[1], both)
            result[c, pl.ds(2 * i, length, stride=PITCH), :] = out[:, :LANES]
            result[c, pl.ds(2 * i + 1, length, stride=PITCH), :] = out[:, LANES:]
        for z in range(length):
            out_ref[z, c] = result[c, z * PITCH : z * PITCH + rows, :].astype(BF16)


def along_z(table, block, after):
    length, comps = block.shape[:2]
    return pl.pallas_call(
        along_z_kernel,
        out_shape=(
            jax.ShapeDtypeStruct(block.shape, BF16),
            jax.ShapeDtypeStruct((8, LANES), F32),
        ),
        in_specs=[whole()] * 2 + [whole(pl.ANY)] * len(after),
        out_specs=(whole(), whole()),
        scratch_shapes=[pltpu.VMEM((comps, (length + 1) * PITCH, LANES), F32)] * 2,
        compiler_params=pltpu.CompilerParams(vmem_limit_bytes=VMEM_LIMIT),
        cost_estimate=pl.CostEstimate(
            flops=4 * length * block.size, bytes_accessed=4 * block.size, transcendentals=0
        ),
        name="along_z",
    )(table, block, *after)


def select_matrix(facts, length):
    column = lax.broadcasted_iota(jnp.int32, (length, LANES), 0).astype(F32)
    return jnp.where(column == facts[0:1], 1.0, 0.0).astype(BF16)


def heap_matrix():
    lane = lax.broadcasted_iota(jnp.int32, (HEAP, LANES), 1)
    atom = lax.broadcasted_iota(jnp.int32, (HEAP, LANES), 0)
    return jnp.where(lane // PAD == atom, 1.0, 0.0).astype(F32)


def read_rows(cargo_refs, facts, rows_ref, sem, reach, stretch):
    heaps = len(cargo_refs)
    for d in range(reach):
        for r in range(heaps):
            block = cargo_refs[r][(d + 1) * stretch - PAD : (d + 1) * stretch, :].astype(F32)
            facts[d * heaps + r] = block
    rows = jnp.concatenate([facts[i, 1:2] for i in range(reach * heaps)], axis=0)
    rows_ref[0][...] = rows.astype(jnp.int32)
    copy = pltpu.make_async_copy(rows_ref[0], rows_ref[1], sem)
    copy.start()
    return copy


def read_weights(cargo_ref, at, count, weights):
    weights[0:count, :] = cargo_ref[pl.ds(pl.multiple_of(at, 16), count), :].astype(F32)


def box_weight(weights, p):
    return jnp.concatenate(
        [weights[(p * SLAB_PLANES + z) * BOX : (p * SLAB_PLANES + z) * BOX + PAD, :] for z in range(SLAB_PLANES)],
        axis=0,
    )


def project_kernel(wave_ref, *refs, heaps, reach, nproj):
    cargo_refs = refs[:heaps]
    out_ref, field, sums, weights, facts, rows_vmem, rows_smem, sem = refs[heaps:]
    planes, length = wave_ref.shape[0], wave_ref.shape[1]
    parts = planes // SLAB_PLANES
    count = nproj * SLAB_PLANES * BOX
    stretch = count + PAD
    size = SLAB_PLANES * PAD
    copy = read_rows(cargo_refs, facts, (rows_vmem, rows_smem), sem, reach, stretch)
    for i in range(planes):
        for half in range(2):
            part = wave_ref[i, :, half * LANES : (half + 1) * LANES].astype(F32)
            field[i, half, 0:length, :] = part
            field[i, half, length : length + PAD, :] = part[0:PAD]
    weights[count : count + PAD, :] = jnp.zeros((PAD, LANES), F32)
    lane = lax.broadcasted_iota(jnp.int32, (planes * PAD, LANES), 1)
    line = lax.broadcasted_iota(jnp.int32, (planes * PAD, LANES), 0)
    lane = jnp.where(line % PAD < BOX, lane // PAD, -1)
    copy.wait()

    for heap in range(heaps):

        def step(d, carry, heap=heap):
            index = d * heaps + heap
            select = select_matrix(facts[index], length)
            taken = jnp.zeros((planes * PAD, LANES), F32)
            for a in range(HEAP):
                y0 = rows_smem[index, a * PAD]
                left = field[:, 0, pl.ds(y0, PAD), :].reshape(planes * PAD, LANES)
                right = field[:, 1, pl.ds(y0, PAD), :].reshape(planes * PAD, LANES)
                window = jnp.concatenate([left, right], axis=1).astype(BF16)
                taken = jnp.where(lane == a, dot(window, select), taken)
            read_weights(cargo_refs[heap], d * stretch, count, weights)
            lines = []
            for p in range(nproj):
                weight = box_weight(weights, p)
                for part in range(parts):
                    product = weight * taken[part * size : (part + 1) * size]
                    lines.append(jnp.sum(product, axis=0, keepdims=True))
            at = pl.multiple_of(index * nproj * parts, 8)
            sums[pl.ds(at, nproj * parts), :] = jnp.concatenate(lines, axis=0)
            return carry

        lax.fori_loop(0, reach, step, 0)
    per_reach = heaps * nproj * parts
    for d in range(reach):
        out_ref[d] = dot(
            heap_matrix(), sums[d * per_reach : (d + 1) * per_reach, :], NT, HIGHEST
        )


def cargo_scratch(groups, nproj):
    return [
        pltpu.VMEM((nproj * SLAB_PLANES * BOX + PAD, LANES), F32),
        pltpu.VMEM((groups, PAD, LANES), F32),
        pltpu.VMEM((groups, LANES), jnp.int32),
        pltpu.SMEM((groups, LANES), jnp.int32),
        pltpu.SemaphoreType.DMA,
    ]


def project(wave, cargo, reach, nproj):
    heaps = len(cargo)
    planes, length, _ = wave.shape
    parts = planes // SLAB_PLANES
    return pl.pallas_call(
        functools.partial(project_kernel, heaps=heaps, reach=reach, nproj=nproj),
        out_shape=jax.ShapeDtypeStruct((reach, HEAP, heaps * nproj * parts), F32),
        in_specs=[whole()] * (1 + heaps),
        out_specs=whole(),
        scratch_shapes=[
            pltpu.VMEM((planes, 2, length + PAD, LANES), F32),
            pltpu.VMEM((reach * heaps * nproj * parts, LANES), F32),
            *cargo_scratch(reach * heaps, nproj),
        ],
        compiler_params=pltpu.CompilerParams(vmem_limit_bytes=VMEM_LIMIT),
        cost_estimate=pl.CostEstimate(
            flops=33_000_000_000, bytes_accessed=5_000_000, transcendentals=0
        ),
        name="project",
    )(wave, *cargo)


def local_kernel(mix_ref, table_ref, wave_ref, *refs, heaps, reach, nproj):
    cargo_refs, well_refs = refs[:heaps], refs[heaps : 2 * heaps]
    mine_ref, pair_ref, above_ref, below_ref, far_ref, _, out_ref = refs[2 * heaps : 2 * heaps + 7]
    total, spread, well, weights, facts, rows_vmem, rows_smem, sem = refs[2 * heaps + 7 :]
    planes, length = wave_ref.shape[0], wave_ref.shape[1]
    parts = planes // SLAB_PLANES
    count = nproj * SLAB_PLANES * BOX
    stretch = count + PAD
    size = SLAB_PLANES * PAD
    per_reach = heaps * nproj * parts
    share = length // heaps
    copy = read_rows(cargo_refs, facts, (rows_vmem, rows_smem), sem, reach, stretch)

    for r in range(heaps):
        place = lax.rem(lax.axis_index("band") + r, heaps) * share
        for half in range(2):
            for z in range(SLAB_PLANES):
                at = (half * SLAB_PLANES + z) * share
                well[half, z, pl.ds(pl.multiple_of(place, 16), share), :] = well_refs[r][at : at + share, :].astype(F32)

    def fill(i, carry):
        wave = wave_ref[i]
        value = dot(wave, table_ref[0]) + dot(wave, table_ref[1])
        value += dot(table_ref[0], wave) + dot(table_ref[1], wave)
        wide = wave.astype(F32)
        for half in range(2):
            at = slice(half * LANES, (half + 1) * LANES)
            potential = well[half, lax.rem(i, SLAB_PLANES)]
            total[i, half, 0:length, :] = value[:, at] + potential * wide[:, at]
            total[i, half, length : length + PAD, :] = jnp.zeros((PAD, LANES), F32)
        return carry

    lax.fori_loop(0, planes, fill, 0)
    even = [far_ref, below_ref.at[0], below_ref.at[1], mine_ref, pair_ref.at[1], above_ref.at[0], above_ref.at[1]]
    odd = [below_ref.at[0], below_ref.at[1], pair_ref.at[0], mine_ref, above_ref.at[0], above_ref.at[1], far_ref]
    is_even = lax.rem(lax.axis_index("slab"), 2) == 0
    for e in range(reach):
        full = None
        for d in range(reach):
            at = reach - 1 + d - e
            value = jnp.where(is_even, even[at][d], odd[at][d])
            full = value if full is None else full + value
        coefficients = dot(full, mix_ref[...], None, HIGHEST)
        spread[e * per_reach : (e + 1) * per_reach, :] = dot(
            coefficients, heap_matrix(), TN, HIGHEST
        )
    weights[count : count + PAD, :] = jnp.zeros((PAD, LANES), F32)
    lane = lax.broadcasted_iota(jnp.int32, (planes * PAD, LANES), 1)
    line = lax.broadcasted_iota(jnp.int32, (planes * PAD, LANES), 0)
    lane = jnp.where(line % PAD < BOX, lane // PAD, -1)
    copy.wait()

    for heap in range(heaps):

        def step(d, carry, heap=heap):
            index = d * heaps + heap
            select = select_matrix(facts[index], length)
            at = pl.multiple_of(index * nproj * parts, 8)
            lines = spread[pl.ds(at, nproj * parts), :] * facts[index, 2:3]
            read_weights(cargo_refs[heap], d * stretch, count, weights)
            blocks = [jnp.zeros((size, LANES), F32) for _ in range(parts)]
            for p in range(nproj):
                weight = box_weight(weights, p)
                for part in range(parts):
                    at = p * parts + part
                    blocks[part] = blocks[part] + weight * lines[at : at + 1, :]
            blocks = jnp.concatenate(blocks, axis=0)
            for a in range(HEAP):
                y0 = rows_smem[index, a * PAD]
                one = jnp.where(lane == a, blocks, 0.0).astype(BF16)
                placed = dot(one, select, NT)
                for half in range(2):
                    part = placed[:, half * LANES : (half + 1) * LANES]
                    total[:, half, pl.ds(y0, PAD), :] += part.reshape(planes, PAD, LANES)
            return carry

        lax.fori_loop(0, reach, step, 0)

    def finish(i, carry):
        for half in range(2):
            at = slice(half * LANES, (half + 1) * LANES)
            first = total[i, half, 0:PAD, :] + total[i, half, length : length + PAD, :]
            out_ref[i, 0:PAD, at] = first.astype(BF16)
            out_ref[i, PAD:length, at] = total[i, half, PAD:length, :].astype(BF16)
        return carry

    lax.fori_loop(0, planes, finish, 0)


def local_part(mix, table, wave, cargo, wells, exchanged, after, nproj):
    heaps = len(cargo)
    planes, length, _ = wave.shape
    parts = planes // SLAB_PLANES
    reach = exchanged[0].shape[0]
    return pl.pallas_call(
        functools.partial(local_kernel, heaps=heaps, reach=reach, nproj=nproj),
        out_shape=jax.ShapeDtypeStruct(wave.shape, BF16),
        in_specs=[whole()] * (3 + 2 * heaps + len(exchanged)) + [whole(pl.ANY)],
        out_specs=whole(),
        scratch_shapes=[
            pltpu.VMEM((planes, 2, length + PAD, LANES), F32),
            pltpu.VMEM((reach * heaps * nproj * parts, LANES), F32),
            pltpu.VMEM((2, SLAB_PLANES, length, LANES), F32),
            *cargo_scratch(reach * heaps, nproj),
        ],
        compiler_params=pltpu.CompilerParams(vmem_limit_bytes=VMEM_LIMIT),
        cost_estimate=pl.CostEstimate(
            flops=10_000_000_000, bytes_accessed=10_000_000, transcendentals=0
        ),
        name="local",
    )(mix, table, wave, *cargo, *wells, *exchanged, after)


def gather_rows(nproj):
    size = SLAB_PLANES * BOX * nproj
    table = np.zeros((size, size), np.float32)
    for p in range(nproj):
        for z in range(SLAB_PLANES):
            for j in range(BOX):
                table[(p * SLAB_PLANES + z) * BOX + j, (z * BOX + j) * nproj + p] = 1.0
    return jnp.asarray(table, BF16)


def frame_kernel(
    box_ref, count_ref, projectors_ref, order_ref, wave_ref, send_ref, *refs
):
    out_refs, scratch = refs[:-10], refs[-10:]
    dense, share_ref, order, done, field, packed, fetch_sem, in_sem, out_sem, done_sem = scratch
    bands, row_blocks, columns, slab_planes, comps = packed.shape[:5]
    heap, nproj, cells = share_ref.shape
    band, anchor = lax.axis_index("band"), lax.axis_index("slab") * SLAB_PLANES
    fetch = pltpu.make_async_copy(
        projectors_ref.at[pl.ds(band * heap, heap)], share_ref, fetch_sem.at[0]
    )
    fetch.start()
    fetch_order = pltpu.make_async_copy(order_ref, order, fetch_sem.at[1])
    count = in_sem.shape[0]
    step = row_blocks // count
    loads, stores = [], []
    for i in range(count):
        lines = slice(i * step * 16, (i + 1) * step * 16)
        at = slice(i * step, (i + 1) * step)
        loads.append(pltpu.make_async_copy(wave_ref.at[:, lines], field.at[:, lines], in_sem.at[i]))
        stores.append(pltpu.make_async_copy(packed.at[:, at], send_ref.at[:, at], out_sem.at[i]))
        loads[i].start()
    fetch_order.start()
    fetch.wait()

    lane = lax.broadcasted_iota(jnp.int32, (nproj, LANES), 1)
    for a in range(heap):
        values = share_ref[a].astype(F32)
        tiles = [values[:, t : min(t + LANES, cells)] for t in range(0, cells, LANES)]
        gap = LANES - tiles[-1].shape[1]
        if gap:
            tiles[-1] = jnp.concatenate([tiles[-1], jnp.zeros((nproj, gap), F32)], axis=1)
        mine = (lane // PAD == a) & (lane % PAD < BOX)
        for m in range(cells // BOX):
            tile, skip = m * BOX // LANES, m * BOX % LANES
            source = tiles[tile]
            if skip + BOX > LANES:
                source = jnp.where(lane >= skip, source, tiles[tile + 1])
            shift = (a * PAD - skip) % LANES
            if shift:
                source = pltpu.roll(source, shift, 1)
            at = (m // BOX, slice(m % BOX * nproj, (m % BOX + 1) * nproj))
            dense[at] = jnp.where(mine, source, dense[at] if a else 0.0)

    for i in range(count):
        loads[i].wait()
        for r in range(i * step, (i + 1) * step):
            for b in range(bands):
                for c in range(comps):
                    for z in range(slab_planes):
                        plane = (b * comps + c) * slab_planes + z
                        for h in range(columns):
                            packed[b, r, h, z, c] = field[
                                plane, r * 16 : (r + 1) * 16, h * LANES : (h + 1) * LANES
                            ]
        stores[i].start()

    lane = lax.broadcasted_iota(jnp.int32, (1, LANES), 1)
    offset = jnp.zeros((1, LANES), jnp.int32)
    row0 = jnp.zeros((1, LANES), jnp.int32)
    column0 = jnp.zeros((1, LANES), jnp.int32)
    live = jnp.zeros((1, LANES), F32)
    for a in range(heap):
        slot = band * heap + a
        mine = lane // PAD == a
        offset = jnp.where(mine, box_ref[0, slot] - anchor, offset)
        row0 = jnp.where(mine, box_ref[1, slot], row0)
        column0 = jnp.where(mine, box_ref[2, slot], column0)
        live = jnp.where(mine, jnp.where(slot < count_ref[0], 1.0, 0.0), live)
    k = lane % PAD
    target = jnp.where(k < BOX, (column0 + k) % NG, -1)
    facts = jnp.concatenate(
        [target.astype(F32), row0.astype(F32), live, jnp.zeros((PAD - 3, LANES), F32)], axis=0
    ).astype(BF16)

    rows = nproj * SLAB_PLANES * BOX
    fetch_order.wait()
    for d in range(len(out_refs)):
        planes = []
        for z in range(SLAB_PLANES):
            f = d * SLAB_PLANES + z
            framed = jnp.zeros((BOX * nproj, LANES), F32)
            for o in range(SLAB_PLANES):
                if 0 <= f - o < BOX:
                    framed = jnp.where(offset == o, dense[f - o], framed)
            planes.append(framed)
        planes = jnp.concatenate(planes, axis=0).astype(BF16)
        done[d, 0:rows, :] = dot(order[...], planes).astype(BF16)
        done[d, rows : rows + PAD, :] = facts
        stores.append(
            pltpu.make_async_copy(done.at[d], out_refs[d].at[0 : rows + PAD], done_sem.at[d])
        )
        stores[-1].start()
    for store in stores:
        store.wait()


def frame(projectors, atom_box, atom_count, wave, bands):
    _, nproj, cells = projectors.shape
    planes, length, _ = wave.shape
    comps = planes // SLAB_PLANES // bands
    reach = (BOX + SLAB_PLANES) // SLAB_PLANES
    order = gather_rows(nproj)
    rows = nproj * SLAB_PLANES * BOX + PAD
    shape = jax.ShapeDtypeStruct((rows, LANES), BF16)
    send = (bands, length // 16, length // LANES, SLAB_PLANES, comps, 16, LANES)
    count = 4
    return pl.pallas_call(
        frame_kernel,
        out_shape=(
            jax.ShapeDtypeStruct(send, BF16),
            jax.ShapeDtypeStruct((reach * rows, LANES), BF16),
        )
        + (shape,) * (reach - 1),
        in_specs=[whole(pltpu.SMEM)] * 2 + [whole(pltpu.HBM)] * 3,
        out_specs=(whole(pltpu.HBM),) * (1 + reach),
        scratch_shapes=[
            pltpu.VMEM((BOX, nproj * BOX, LANES), F32),
            pltpu.VMEM((HEAP, nproj, cells), BF16),
            pltpu.VMEM(order.shape, BF16),
            pltpu.VMEM((reach, rows, LANES), BF16),
            pltpu.VMEM(wave.shape, BF16),
            pltpu.VMEM(send, BF16),
            pltpu.SemaphoreType.DMA((2,)),
            pltpu.SemaphoreType.DMA((count,)),
            pltpu.SemaphoreType.DMA((count,)),
            pltpu.SemaphoreType.DMA((reach,)),
        ],
        compiler_params=pltpu.CompilerParams(vmem_limit_bytes=VMEM_MOST),
        cost_estimate=pl.CostEstimate(
            flops=1_000_000_000, bytes_accessed=9_000_000, transcendentals=0
        ),
        name="frame",
    )(atom_box, atom_count, projectors, order, wave)


def gate_kernel(*refs):
    pass


def gate(block, after):
    return pl.pallas_call(
        gate_kernel,
        out_shape=jax.ShapeDtypeStruct(block.shape, block.dtype),
        in_specs=[whole(pltpu.HBM)] + [whole(pl.ANY)] * len(after),
        out_specs=whole(pltpu.HBM),
        input_output_aliases={0: 0},
        compiler_params=pltpu.CompilerParams(vmem_limit_bytes=VMEM_MOST),
        name="gate",
    )(block, *after)


def join_kernel(local_ref, arrived_ref, out_ref, near, here, there, near_sem, in_sem, out_sem):
    bands, rows, columns, slab_planes, comps = arrived_ref.shape[:5]
    count = in_sem.shape[0]
    step = rows // count
    loads, stores = [], []
    for i in range(count):
        at = slice(i * step, (i + 1) * step)
        lines = slice(i * step * 16, (i + 1) * step * 16)
        loads.append(pltpu.make_async_copy(local_ref.at[:, lines], near.at[:, lines], near_sem.at[i]))
        loads.append(pltpu.make_async_copy(arrived_ref.at[:, at], here.at[:, at], in_sem.at[i]))
        stores.append(pltpu.make_async_copy(there.at[:, lines], out_ref.at[:, lines], out_sem.at[i]))
    for load in loads:
        load.start()
    for i in range(count):
        loads[2 * i].wait()
        loads[2 * i + 1].wait()
        for r in range(i * step, (i + 1) * step):
            for b in range(bands):
                for c in range(comps):
                    for z in range(slab_planes):
                        plane = (b * comps + c) * slab_planes + z
                        for h in range(columns):
                            at = (plane, slice(r * 16, (r + 1) * 16), slice(h * LANES, (h + 1) * LANES))
                            value = near[at].astype(F32) + here[b, r, h, z, c].astype(F32)
                            there[at] = value.astype(BF16)
        stores[i].start()
    for store in stores:
        store.wait()


def join(local, arrived):
    count = 4
    return pl.pallas_call(
        join_kernel,
        out_shape=jax.ShapeDtypeStruct(local.shape, BF16),
        in_specs=[whole(pltpu.HBM), whole(pltpu.HBM)],
        out_specs=whole(pltpu.HBM),
        scratch_shapes=[
            pltpu.VMEM(local.shape, BF16),
            pltpu.VMEM(arrived.shape, BF16),
            pltpu.VMEM(local.shape, BF16),
            pltpu.SemaphoreType.DMA((count,)),
            pltpu.SemaphoreType.DMA((count,)),
            pltpu.SemaphoreType.DMA((count,)),
        ],
        compiler_params=pltpu.CompilerParams(vmem_limit_bytes=VMEM_MOST),
        cost_estimate=pl.CostEstimate(
            flops=2 * local.size, bytes_accessed=6 * local.size, transcendentals=0
        ),
        name="join",
    )(local, arrived)


def ahead(block, distance, axis="slab"):
    size = lax.axis_size(axis)
    return lax.ppermute(block, axis, [(i, (i + distance) % size) for i in range(size)])


def shards(wavefunctions, potential, atom_box, atom_count, projectors, coupling):
    bands, comps, slab_planes, length, _ = wavefunctions.shape
    parts = bands * comps
    planes = parts * slab_planes
    slabs = lax.axis_size("slab")
    heaps = lax.axis_size("band")
    nproj = projectors.shape[1]
    table = kinetic_table(length)
    wave = wavefunctions.reshape(planes, length, length)

    send, cargo, *framed = frame(projectors, atom_box, atom_count, wave, bands)
    reach = len(framed) + 1
    arrived = [ahead(framed[d - 1], d) for d in range(1, reach)]

    send = gate(send, arrived[:1]).reshape(slabs, slab_planes * comps, 16, LANES)
    columns = lax.all_to_all(send, "slab", split_axis=0, concat_axis=0, tiled=True)

    rows = arrived[0].shape[0]
    for d in range(1, reach):
        cargo = lax.dynamic_update_slice_in_dim(cargo, arrived[d - 1], d * rows, 0)
    cargo = [cargo] + [ahead(cargo, -r, "band") for r in range(1, heaps)]
    well = potential.astype(BF16).reshape(slab_planes, length // heaps, 2, LANES)
    well = well.transpose(2, 0, 1, 3).reshape(-1, LANES)
    wells = [well] + [ahead(well, -r, "band") for r in range(1, heaps)]

    partial = project(wave, cargo, reach, nproj)
    other = lax.ppermute(partial, "slab", [(i, i ^ 1) for i in range(slabs)])
    even = lax.axis_index("slab") % 2 == 0
    pair = jnp.stack([jnp.where(even, partial, other), jnp.where(even, other, partial)])
    above = ahead(pair, -2)
    below = ahead(pair, 2)
    far = lax.ppermute(
        partial, "slab", [(i, (i + 3 if i % 2 else i - 3) % slabs) for i in range(slabs)]
    )

    symmetric = (coupling + coupling.T) * 0.5
    mix = jnp.einsum(
        "gh,pq,bc->gqbhpc", jnp.eye(heaps, dtype=F32), symmetric, jnp.eye(parts, dtype=F32),
        precision=HIGHEST,
    ).reshape(heaps * nproj * parts, heaps * nproj * parts)

    exchanged = [partial, pair, above, below, far]
    columns, token = along_z(table, columns.reshape(length, comps, 16, LANES), exchanged[2:])
    local = local_part(mix, table, wave, cargo, wells, exchanged, token, nproj)
    columns = columns.reshape(slabs, slab_planes * comps, 16, LANES)
    back = lax.all_to_all(columns, "slab", split_axis=0, concat_axis=0, tiled=True)
    back = back.reshape(bands, length // 16, length // LANES, slab_planes, comps, 16, LANES)
    return join(local, back).reshape(wavefunctions.shape)


def solution(mesh):
    placed = (
        P("band", None, "slab", None, None),
        P("slab", "band", None),
        P(None, "slab"),
        P("slab"),
        P("slab", None, None),
        P(),
    )
    return jax.shard_map(
        shards,
        mesh=mesh,
        in_specs=placed,
        out_specs=P("band", None, "slab", None, None),
        check_vma=False,
    )
```

```python
import functools

import numpy as np

import jax
import jax.numpy as jnp
from jax import lax
from jax.experimental import pallas as pl
from jax.experimental.pallas import tpu as pltpu
from jax.sharding import PartitionSpec as P

NG = 256
BOX = 12
SLAB_PLANES = 4
PAD = 16
PITCH = 20
LANES = 128
HEAP = LANES // PAD
F32 = jnp.float32
BF16 = jnp.bfloat16
HIGHEST = lax.Precision.HIGHEST
VMEM_LIMIT = 28 * 1024 * 1024
VMEM_MOST = 62 * 1024 * 1024
NT = (((1,), (1,)), ((), ()))
TN = (((0,), (0,)), ((), ()))


def kinetic_table(length):
    counter = np.arange(length)
    signed = np.where(counter < length // 2, counter, counter - length).astype(np.float64)
    angle = 2.0 * np.pi * ((counter[:, None] * counter[None, :]) % length) / length
    spectrum = signed**2 / (3.0 * (length // 2) ** 2)
    row = (np.cos(angle) * spectrum[None, :]).sum(1) / length
    table = row[(counter[:, None] - counter[None, :]) % length]
    high = jnp.asarray(table, F32).astype(BF16)
    low = (jnp.asarray(table, F32) - high.astype(F32)).astype(BF16)
    return jnp.stack([high, low])


def whole(space=pltpu.VMEM):
    return pl.BlockSpec(memory_space=space)


def dot(a, b, dims=None, precision=None):
    if dims is None:
        dims = (((1,), (0,)), ((), ()))
    return lax.dot_general(a, b, dims, precision=precision, preferred_element_type=F32)


def circulant(length):
    column = lax.broadcasted_iota(jnp.int32, (8, length), 1)
    near = jnp.minimum(column, length - column)
    scale = 1.0 / (3.0 * (length // 2) ** 2)
    sine = jnp.sin(near.astype(F32) * (np.pi / length))
    sign = jnp.where(near % 2 == 0, 0.5 * scale, -0.5 * scale)
    row = sign / jnp.where(near == 0, 1.0, sine * sine)
    row = jnp.where(near == 0, scale * (length * length + 2) / 12.0, row)
    full = jnp.broadcast_to(row[0:1], (length, length))
    full = pltpu.roll(full, 0, 1, stride=1, stride_axis=0)
    high = full.astype(BF16)
    return high, (full - high.astype(F32)).astype(BF16)


def along_z_kernel(in_ref, *refs):
    out_ref, token_ref, wide, result = refs[-4:]
    token_ref[...] = jnp.zeros_like(token_ref)
    length, comps, rows = in_ref.shape[:3]
    high, low = circulant(length)
    for c in range(comps):
        for z in range(length):
            wide[c, z * PITCH : z * PITCH + rows, :] = in_ref[z, c].astype(F32)
        for i in range(rows // 2):
            left = wide[c, pl.ds(2 * i, length, stride=PITCH), :]
            right = wide[c, pl.ds(2 * i + 1, length, stride=PITCH), :]
            both = jnp.concatenate([left, right], axis=1).astype(BF16)
            out = dot(high, both) + dot(low, both)
            result[c, pl.ds(2 * i, length, stride=PITCH), :] = out[:, :LANES]
            result[c, pl.ds(2 * i + 1, length, stride=PITCH), :] = out[:, LANES:]
        for z in range(length):
            out_ref[z, c] = result[c, z * PITCH : z * PITCH + rows, :].astype(BF16)


def along_z(block, after):
    length, comps = block.shape[:2]
    return pl.pallas_call(
        along_z_kernel,
        out_shape=(
            jax.ShapeDtypeStruct(block.shape, BF16),
            jax.ShapeDtypeStruct((8, LANES), F32),
        ),
        in_specs=[whole()] + [whole(pl.ANY)] * len(after),
        out_specs=(whole(), whole()),
        scratch_shapes=[pltpu.VMEM((comps, (length + 1) * PITCH, LANES), F32)] * 2,
        compiler_params=pltpu.CompilerParams(vmem_limit_bytes=VMEM_LIMIT),
        cost_estimate=pl.CostEstimate(
            flops=4 * length * block.size, bytes_accessed=4 * block.size, transcendentals=0
        ),
        name="along_z",
    )(block, *after)


def select_matrix(facts, length):
    column = lax.broadcasted_iota(jnp.int32, (length, LANES), 0).astype(F32)
    return jnp.where(column == facts[0:1], 1.0, 0.0).astype(BF16)


def heap_matrix():
    lane = lax.broadcasted_iota(jnp.int32, (HEAP, LANES), 1)
    atom = lax.broadcasted_iota(jnp.int32, (HEAP, LANES), 0)
    return jnp.where(lane // PAD == atom, 1.0, 0.0).astype(F32)


def read_rows(cargo_refs, facts, rows_ref, sem, reach, stretch):
    heaps = len(cargo_refs)
    for d in range(reach):
        for r in range(heaps):
            block = cargo_refs[r][(d + 1) * stretch - PAD : (d + 1) * stretch, :].astype(F32)
            facts[d * heaps + r] = block
    rows = jnp.concatenate([facts[i, 1:2] for i in range(reach * heaps)], axis=0)
    rows_ref[0][...] = rows.astype(jnp.int32)
    copy = pltpu.make_async_copy(rows_ref[0], rows_ref[1], sem)
    copy.start()
    return copy


def read_weights(cargo_ref, at, count, weights):
    weights[0:count, :] = cargo_ref[pl.ds(pl.multiple_of(at, 16), count), :].astype(F32)


def box_weight(weights, p):
    return jnp.concatenate(
        [weights[(p * SLAB_PLANES + z) * BOX : (p * SLAB_PLANES + z) * BOX + PAD, :] for z in range(SLAB_PLANES)],
        axis=0,
    )


def project_kernel(wave_ref, *refs, heaps, reach, nproj):
    cargo_refs = refs[:heaps]
    out_ref, field, sums, weights, facts, rows_vmem, rows_smem, sem = refs[heaps:]
    planes, length = wave_ref.shape[0], wave_ref.shape[1]
    parts = planes // SLAB_PLANES
    count = nproj * SLAB_PLANES * BOX
    stretch = count + PAD
    size = SLAB_PLANES * PAD
    copy = read_rows(cargo_refs, facts, (rows_vmem, rows_smem), sem, reach, stretch)
    for i in range(planes):
        for half in range(2):
            part = wave_ref[i, :, half * LANES : (half + 1) * LANES].astype(F32)
            field[i, half, 0:length, :] = part
            field[i, half, length : length + PAD, :] = part[0:PAD]
    weights[count : count + PAD, :] = jnp.zeros((PAD, LANES), F32)
    lane = lax.broadcasted_iota(jnp.int32, (planes * PAD, LANES), 1)
    line = lax.broadcasted_iota(jnp.int32, (planes * PAD, LANES), 0)
    lane = jnp.where(line % PAD < BOX, lane // PAD, -1)
    copy.wait()

    for heap in range(heaps):

        def step(d, carry, heap=heap):
            index = d * heaps + heap
            select = select_matrix(facts[index], length)
            taken = jnp.zeros((planes * PAD, LANES), F32)
            for a in range(HEAP):
                y0 = rows_smem[index, a * PAD]
                left = field[:, 0, pl.ds(y0, PAD), :].reshape(planes * PAD, LANES)
                right = field[:, 1, pl.ds(y0, PAD), :].reshape(planes * PAD, LANES)
                window = jnp.concatenate([left, right], axis=1).astype(BF16)
                taken = jnp.where(lane == a, dot(window, select), taken)
            read_weights(cargo_refs[heap], d * stretch, count, weights)
            lines = []
            for p in range(nproj):
                weight = box_weight(weights, p)
                for part in range(parts):
                    product = weight * taken[part * size : (part + 1) * size]
                    lines.append(jnp.sum(product, axis=0, keepdims=True))
            at = pl.multiple_of(index * nproj * parts, 8)
            sums[pl.ds(at, nproj * parts), :] = jnp.concatenate(lines, axis=0)
            return carry

        lax.fori_loop(0, reach, step, 0)
    per_reach = heaps * nproj * parts
    for d in range(reach):
        out_ref[d] = dot(
            heap_matrix(), sums[d * per_reach : (d + 1) * per_reach, :], NT, HIGHEST
        )


def cargo_scratch(groups, nproj):
    return [
        pltpu.VMEM((nproj * SLAB_PLANES * BOX + PAD, LANES), F32),
        pltpu.VMEM((groups, PAD, LANES), F32),
        pltpu.VMEM((groups, LANES), jnp.int32),
        pltpu.SMEM((groups, LANES), jnp.int32),
        pltpu.SemaphoreType.DMA,
    ]


def project(wave, cargo, reach, nproj):
    heaps = len(cargo)
    planes, length, _ = wave.shape
    parts = planes // SLAB_PLANES
    return pl.pallas_call(
        functools.partial(project_kernel, heaps=heaps, reach=reach, nproj=nproj),
        out_shape=jax.ShapeDtypeStruct((reach, HEAP, heaps * nproj * parts), F32),
        in_specs=[whole()] * (1 + heaps),
        out_specs=whole(),
        scratch_shapes=[
            pltpu.VMEM((planes, 2, length + PAD, LANES), F32),
            pltpu.VMEM((reach * heaps * nproj * parts, LANES), F32),
            *cargo_scratch(reach * heaps, nproj),
        ],
        compiler_params=pltpu.CompilerParams(vmem_limit_bytes=VMEM_LIMIT),
        cost_estimate=pl.CostEstimate(
            flops=33_000_000_000, bytes_accessed=5_000_000, transcendentals=0
        ),
        name="project",
    )(wave, *cargo)


def local_kernel(mix_ref, table_ref, wave_ref, *refs, heaps, reach, nproj):
    cargo_refs, well_refs = refs[:heaps], refs[heaps : 2 * heaps]
    mine_ref, pair_ref, above_ref, below_ref, far_ref, _, out_ref = refs[2 * heaps : 2 * heaps + 7]
    total, spread, well, weights, facts, rows_vmem, rows_smem, sem = refs[2 * heaps + 7 :]
    planes, length = wave_ref.shape[0], wave_ref.shape[1]
    parts = planes // SLAB_PLANES
    count = nproj * SLAB_PLANES * BOX
    stretch = count + PAD
    size = SLAB_PLANES * PAD
    per_reach = heaps * nproj * parts
    share = length // heaps
    copy = read_rows(cargo_refs, facts, (rows_vmem, rows_smem), sem, reach, stretch)

    for r in range(heaps):
        place = lax.rem(lax.axis_index("band") + r, heaps) * share
        for half in range(2):
            for z in range(SLAB_PLANES):
                at = (half * SLAB_PLANES + z) * share
                well[half, z, pl.ds(pl.multiple_of(place, 16), share), :] = well_refs[r][at : at + share, :].astype(F32)

    def fill(i, carry):
        wave = wave_ref[i]
        value = dot(wave, table_ref[0]) + dot(wave, table_ref[1])
        value += dot(table_ref[0], wave) + dot(table_ref[1], wave)
        wide = wave.astype(F32)
        for half in range(2):
            at = slice(half * LANES, (half + 1) * LANES)
            potential = well[half, lax.rem(i, SLAB_PLANES)]
            total[i, half, 0:length, :] = value[:, at] + potential * wide[:, at]
            total[i, half, length : length + PAD, :] = jnp.zeros((PAD, LANES), F32)
        return carry

    lax.fori_loop(0, planes, fill, 0)
    even = [far_ref, below_ref.at[0], below_ref.at[1], mine_ref, pair_ref.at[1], above_ref.at[0], above_ref.at[1]]
    odd = [below_ref.at[0], below_ref.at[1], pair_ref.at[0], mine_ref, above_ref.at[0], above_ref.at[1], far_ref]
    is_even = lax.rem(lax.axis_index("slab"), 2) == 0
    for e in range(reach):
        full = None
        for d in range(reach):
            at = reach - 1 + d - e
            value = jnp.where(is_even, even[at][d], odd[at][d])
            full = value if full is None else full + value
        coefficients = dot(full, mix_ref[...], None, HIGHEST)
        spread[e * per_reach : (e + 1) * per_reach, :] = dot(
            coefficients, heap_matrix(), TN, HIGHEST
        )
    weights[count : count + PAD, :] = jnp.zeros((PAD, LANES), F32)
    lane = lax.broadcasted_iota(jnp.int32, (planes * PAD, LANES), 1)
    line = lax.broadcasted_iota(jnp.int32, (planes * PAD, LANES), 0)
    lane = jnp.where(line % PAD < BOX, lane // PAD, -1)
    copy.wait()

    for heap in range(heaps):

        def step(d, carry, heap=heap):
            index = d * heaps + heap
            select = select_matrix(facts[index], length)
            at = pl.multiple_of(index * nproj * parts, 8)
            lines = spread[pl.ds(at, nproj * parts), :] * facts[index, 2:3]
            read_weights(cargo_refs[heap], d * stretch, count, weights)
            blocks = [jnp.zeros((size, LANES), F32) for _ in range(parts)]
            for p in range(nproj):
                weight = box_weight(weights, p)
                for part in range(parts):
                    at = p * parts + part
                    blocks[part] = blocks[part] + weight * lines[at : at + 1, :]
            blocks = jnp.concatenate(blocks, axis=0)
            for a in range(HEAP):
                y0 = rows_smem[index, a * PAD]
                one = jnp.where(lane == a, blocks, 0.0).astype(BF16)
                placed = dot(one, select, NT)
                for half in range(2):
                    part = placed[:, half * LANES : (half + 1) * LANES]
                    total[:, half, pl.ds(y0, PAD), :] += part.reshape(planes, PAD, LANES)
            return carry

        lax.fori_loop(0, reach, step, 0)

    def finish(i, carry):
        for half in range(2):
            at = slice(half * LANES, (half + 1) * LANES)
            first = total[i, half, 0:PAD, :] + total[i, half, length : length + PAD, :]
            out_ref[i, 0:PAD, at] = first.astype(BF16)
            out_ref[i, PAD:length, at] = total[i, half, PAD:length, :].astype(BF16)
        return carry

    lax.fori_loop(0, planes, finish, 0)


def local_part(mix, table, wave, cargo, wells, exchanged, after, nproj):
    heaps = len(cargo)
    planes, length, _ = wave.shape
    parts = planes // SLAB_PLANES
    reach = exchanged[0].shape[0]
    return pl.pallas_call(
        functools.partial(local_kernel, heaps=heaps, reach=reach, nproj=nproj),
        out_shape=jax.ShapeDtypeStruct(wave.shape, BF16),
        in_specs=[whole()] * (3 + 2 * heaps + len(exchanged)) + [whole(pl.ANY)],
        out_specs=whole(),
        scratch_shapes=[
            pltpu.VMEM((planes, 2, length + PAD, LANES), F32),
            pltpu.VMEM((reach * heaps * nproj * parts, LANES), F32),
            pltpu.VMEM((2, SLAB_PLANES, length, LANES), F32),
            *cargo_scratch(reach * heaps, nproj),
        ],
        compiler_params=pltpu.CompilerParams(vmem_limit_bytes=VMEM_LIMIT),
        cost_estimate=pl.CostEstimate(
            flops=10_000_000_000, bytes_accessed=10_000_000, transcendentals=0
        ),
        name="local",
    )(mix, table, wave, *cargo, *wells, *exchanged, after)


def gather_rows(nproj):
    size = SLAB_PLANES * BOX * nproj
    table = np.zeros((size, size), np.float32)
    for p in range(nproj):
        for z in range(SLAB_PLANES):
            for j in range(BOX):
                table[(p * SLAB_PLANES + z) * BOX + j, (z * BOX + j) * nproj + p] = 1.0
    return jnp.asarray(table, BF16)


def frame_kernel(
    box_ref, count_ref, projectors_ref, order_ref, wave_ref, send_ref, *refs
):
    out_refs, scratch = refs[:-10], refs[-10:]
    dense, share_ref, order, done, field, packed, fetch_sem, in_sem, out_sem, done_sem = scratch
    bands, row_blocks, columns, slab_planes, comps = packed.shape[:5]
    heap, nproj, cells = share_ref.shape
    band, anchor = lax.axis_index("band"), lax.axis_index("slab") * SLAB_PLANES
    fetch = pltpu.make_async_copy(
        projectors_ref.at[pl.ds(band * heap, heap)], share_ref, fetch_sem.at[0]
    )
    fetch.start()
    fetch_order = pltpu.make_async_copy(order_ref, order, fetch_sem.at[1])
    count = in_sem.shape[0]
    step = row_blocks // count
    loads, stores = [], []
    for i in range(count):
        lines = slice(i * step * 16, (i + 1) * step * 16)
        at = slice(i * step, (i + 1) * step)
        loads.append(pltpu.make_async_copy(wave_ref.at[:, lines], field.at[:, lines], in_sem.at[i]))
        stores.append(pltpu.make_async_copy(packed.at[:, at], send_ref.at[:, at], out_sem.at[i]))
        loads[i].start()
    fetch_order.start()
    fetch.wait()

    lane = lax.broadcasted_iota(jnp.int32, (nproj, LANES), 1)
    for a in range(heap):
        values = share_ref[a].astype(F32)
        tiles = [values[:, t : min(t + LANES, cells)] for t in range(0, cells, LANES)]
        gap = LANES - tiles[-1].shape[1]
        if gap:
            tiles[-1] = jnp.concatenate([tiles[-1], jnp.zeros((nproj, gap), F32)], axis=1)
        mine = (lane // PAD == a) & (lane % PAD < BOX)
        for m in range(cells // BOX):
            tile, skip = m * BOX // LANES, m * BOX % LANES
            source = tiles[tile]
            if skip + BOX > LANES:
                source = jnp.where(lane >= skip, source, tiles[tile + 1])
            shift = (a * PAD - skip) % LANES
            if shift:
                source = pltpu.roll(source, shift, 1)
            at = (m // BOX, slice(m % BOX * nproj, (m % BOX + 1) * nproj))
            dense[at] = jnp.where(mine, source, dense[at] if a else 0.0)

    for i in range(count):
        loads[i].wait()
        for r in range(i * step, (i + 1) * step):
            for b in range(bands):
                for c in range(comps):
                    for z in range(slab_planes):
                        plane = (b * comps + c) * slab_planes + z
                        for h in range(columns):
                            packed[b, r, h, z, c] = field[
                                plane, r * 16 : (r + 1) * 16, h * LANES : (h + 1) * LANES
                            ]
        stores[i].start()

    lane = lax.broadcasted_iota(jnp.int32, (1, LANES), 1)
    offset = jnp.zeros((1, LANES), jnp.int32)
    row0 = jnp.zeros((1, LANES), jnp.int32)
    column0 = jnp.zeros((1, LANES), jnp.int32)
    live = jnp.zeros((1, LANES), F32)
    for a in range(heap):
        slot = band * heap + a
        mine = lane // PAD == a
        offset = jnp.where(mine, box_ref[0, slot] - anchor, offset)
        row0 = jnp.where(mine, box_ref[1, slot], row0)
        column0 = jnp.where(mine, box_ref[2, slot], column0)
        live = jnp.where(mine, jnp.where(slot < count_ref[0], 1.0, 0.0), live)
    k = lane % PAD
    target = jnp.where(k < BOX, (column0 + k) % NG, -1)
    facts = jnp.concatenate(
        [target.astype(F32), row0.astype(F32), live, jnp.zeros((PAD - 3, LANES), F32)], axis=0
    ).astype(BF16)

    rows = nproj * SLAB_PLANES * BOX
    fetch_order.wait()
    for d in range(len(out_refs)):
        planes = []
        for z in range(SLAB_PLANES):
            f = d * SLAB_PLANES + z
            framed = jnp.zeros((BOX * nproj, LANES), F32)
            for o in range(SLAB_PLANES):
                if 0 <= f - o < BOX:
                    framed = jnp.where(offset == o, dense[f - o], framed)
            planes.append(framed)
        planes = jnp.concatenate(planes, axis=0).astype(BF16)
        done[d, 0:rows, :] = dot(order[...], planes).astype(BF16)
        done[d, rows : rows + PAD, :] = facts
        stores.append(
            pltpu.make_async_copy(done.at[d], out_refs[d].at[0 : rows + PAD], done_sem.at[d])
        )
        stores[-1].start()
    for store in stores:
        store.wait()


def frame(projectors, atom_box, atom_count, wave, bands):
    _, nproj, cells = projectors.shape
    planes, length, _ = wave.shape
    comps = planes // SLAB_PLANES // bands
    reach = (BOX + SLAB_PLANES) // SLAB_PLANES
    order = gather_rows(nproj)
    rows = nproj * SLAB_PLANES * BOX + PAD
    shape = jax.ShapeDtypeStruct((rows, LANES), BF16)
    send = (bands, length // 16, length // LANES, SLAB_PLANES, comps, 16, LANES)
    count = 4
    return pl.pallas_call(
        frame_kernel,
        out_shape=(
            jax.ShapeDtypeStruct(send, BF16),
            jax.ShapeDtypeStruct((reach * rows, LANES), BF16),
        )
        + (shape,) * (reach - 1),
        in_specs=[whole(pltpu.SMEM)] * 2 + [whole(pltpu.HBM)] * 3,
        out_specs=(whole(pltpu.HBM),) * (1 + reach),
        scratch_shapes=[
            pltpu.VMEM((BOX, nproj * BOX, LANES), F32),
            pltpu.VMEM((HEAP, nproj, cells), BF16),
            pltpu.VMEM(order.shape, BF16),
            pltpu.VMEM((reach, rows, LANES), BF16),
            pltpu.VMEM(wave.shape, BF16),
            pltpu.VMEM(send, BF16),
            pltpu.SemaphoreType.DMA((2,)),
            pltpu.SemaphoreType.DMA((count,)),
            pltpu.SemaphoreType.DMA((count,)),
            pltpu.SemaphoreType.DMA((reach,)),
        ],
        compiler_params=pltpu.CompilerParams(vmem_limit_bytes=VMEM_MOST),
        cost_estimate=pl.CostEstimate(
            flops=1_000_000_000, bytes_accessed=9_000_000, transcendentals=0
        ),
        name="frame",
    )(atom_box, atom_count, projectors, order, wave)


def gate_kernel(*refs):
    pass


def gate(block, after):
    return pl.pallas_call(
        gate_kernel,
        out_shape=jax.ShapeDtypeStruct(block.shape, block.dtype),
        in_specs=[whole(pltpu.HBM)] + [whole(pl.ANY)] * len(after),
        out_specs=whole(pltpu.HBM),
        input_output_aliases={0: 0},
        compiler_params=pltpu.CompilerParams(vmem_limit_bytes=VMEM_MOST),
        name="gate",
    )(block, *after)


def join_kernel(local_ref, arrived_ref, out_ref, near, here, there, near_sem, in_sem, out_sem):
    bands, rows, columns, slab_planes, comps = arrived_ref.shape[:5]
    count = in_sem.shape[0]
    step = rows // count
    loads, stores = [], []
    for i in range(count):
        at = slice(i * step, (i + 1) * step)
        lines = slice(i * step * 16, (i + 1) * step * 16)
        loads.append(pltpu.make_async_copy(local_ref.at[:, lines], near.at[:, lines], near_sem.at[i]))
        loads.append(pltpu.make_async_copy(arrived_ref.at[:, at], here.at[:, at], in_sem.at[i]))
        stores.append(pltpu.make_async_copy(there.at[:, lines], out_ref.at[:, lines], out_sem.at[i]))
    for load in loads:
        load.start()
    for i in range(count):
        loads[2 * i].wait()
        loads[2 * i + 1].wait()
        for r in range(i * step, (i + 1) * step):
            for b in range(bands):
                for c in range(comps):
                    for z in range(slab_planes):
                        plane = (b * comps + c) * slab_planes + z
                        for h in range(columns):
                            at = (plane, slice(r * 16, (r + 1) * 16), slice(h * LANES, (h + 1) * LANES))
                            value = near[at].astype(F32) + here[b, r, h, z, c].astype(F32)
                            there[at] = value.astype(BF16)
        stores[i].start()
    for store in stores:
        store.wait()


def join(local, arrived):
    count = 4
    return pl.pallas_call(
        join_kernel,
        out_shape=jax.ShapeDtypeStruct(local.shape, BF16),
        in_specs=[whole(pltpu.HBM), whole(pltpu.HBM)],
        out_specs=whole(pltpu.HBM),
        scratch_shapes=[
            pltpu.VMEM(local.shape, BF16),
            pltpu.VMEM(arrived.shape, BF16),
            pltpu.VMEM(local.shape, BF16),
            pltpu.SemaphoreType.DMA((count,)),
            pltpu.SemaphoreType.DMA((count,)),
            pltpu.SemaphoreType.DMA((count,)),
        ],
        compiler_params=pltpu.CompilerParams(vmem_limit_bytes=VMEM_MOST),
        cost_estimate=pl.CostEstimate(
            flops=2 * local.size, bytes_accessed=6 * local.size, transcendentals=0
        ),
        name="join",
    )(local, arrived)


def ahead(block, distance, axis="slab"):
    size = lax.axis_size(axis)
    return lax.ppermute(block, axis, [(i, (i + distance) % size) for i in range(size)])


def shards(wavefunctions, potential, atom_box, atom_count, projectors, coupling):
    bands, comps, slab_planes, length, _ = wavefunctions.shape
    parts = bands * comps
    planes = parts * slab_planes
    slabs = lax.axis_size("slab")
    heaps = lax.axis_size("band")
    nproj = projectors.shape[1]
    table = kinetic_table(length)
    wave = wavefunctions.reshape(planes, length, length)

    send, cargo, *framed = frame(projectors, atom_box, atom_count, wave, bands)
    reach = len(framed) + 1
    arrived = [ahead(framed[d - 1], d) for d in range(1, reach)]

    send = gate(send, arrived[:1]).reshape(slabs, slab_planes * comps, 16, LANES)
    columns = lax.all_to_all(send, "slab", split_axis=0, concat_axis=0, tiled=True)

    rows = arrived[0].shape[0]
    for d in range(1, reach):
        cargo = lax.dynamic_update_slice_in_dim(cargo, arrived[d - 1], d * rows, 0)
    cargo = [cargo] + [ahead(cargo, -r, "band") for r in range(1, heaps)]
    well = potential.astype(BF16).reshape(slab_planes, length // heaps, 2, LANES)
    well = well.transpose(2, 0, 1, 3).reshape(-1, LANES)
    wells = [well] + [ahead(well, -r, "band") for r in range(1, heaps)]

    partial = project(wave, cargo, reach, nproj)
    other = lax.ppermute(partial, "slab", [(i, i ^ 1) for i in range(slabs)])
    even = lax.axis_index("slab") % 2 == 0
    pair = jnp.stack([jnp.where(even, partial, other), jnp.where(even, other, partial)])
    above = ahead(pair, -2)
    below = ahead(pair, 2)
    far = lax.ppermute(
        partial, "slab", [(i, (i + 3 if i % 2 else i - 3) % slabs) for i in range(slabs)]
    )

    symmetric = (coupling + coupling.T) * 0.5
    mix = jnp.einsum(
        "gh,pq,bc->gqbhpc", jnp.eye(heaps, dtype=F32), symmetric, jnp.eye(parts, dtype=F32),
        precision=HIGHEST,
    ).reshape(heaps * nproj * parts, heaps * nproj * parts)

    exchanged = [partial, pair, above, below, far]
    columns, token = along_z(columns.reshape(length, comps, 16, LANES), exchanged[2:])
    local = local_part(mix, table, wave, cargo, wells, exchanged, token, nproj)
    columns = columns.reshape(slabs, slab_planes * comps, 16, LANES)
    back = lax.all_to_all(columns, "slab", split_axis=0, concat_axis=0, tiled=True)
    back = back.reshape(bands, length // 16, length // LANES, slab_planes, comps, 16, LANES)
    return join(local, back).reshape(wavefunctions.shape)


def solution(mesh):
    placed = (
        P("band", None, "slab", None, None),
        P("slab", "band", None),
        P(None, "slab"),
        P("slab"),
        P("slab", None, None),
        P(),
    )
    return jax.shard_map(
        shards,
        mesh=mesh,
        in_specs=placed,
        out_specs=P("band", None, "slab", None, None),
        check_vma=False,
    )
```
